256 devices in a mesh: seg: 16 (over x, y_lo, core), sub: 16 (over z, y_hi).
Axes of the slice: x: 4, y: 4 (y_hi: 2, y_lo: 2; y = y_hi * 2 + y_lo), z: 8, core: 2. Of those that a mesh axis runs over, the one named last changes fastest.
Arguments:
- edge_mid: float32 [16, 3, 4096], P('sub', None, 'seg'), may hold values from -1 to 1
- edge_dir: float32 [16, 3, 4096], P('sub', None, 'seg'), may hold values from -6 to 6
- seg_mid: float32 [3, 4096], P(None, 'seg'), may hold values from -1.5 to 1.5
- seg_vec: float32 [3, 4096], P(None, 'seg'), may hold values from -0.09375 to 0.09375
- currents: float32 [128, 4096], P(None, 'seg'), may hold values from -6 to 6
- flexibility: float32 [16, 4096, 4096], P('sub', 'seg'), as said below
- partner: int32 [6, 16], replicated, may hold values from 0 to 15, as said below
- edge_block: int32 [6, 16, 24], P(None, 'sub'), may hold values from 0 to 255, as said below
Outputs:
- multipliers: float32 [16, 6, 384, 128], P('sub', None, 'seg')
- trace: float32 [16, 4096, 128], P('sub', 'seg')
The draws below stay inside these ranges and needn't reach their ends.
Inputs may be any that keep to these rules, and one draw needn't show every extreme that they name: For each round the subdomains are matched in pairs: partner[r, j] != j and partner[r, partner[r, j]] == j. For each subdomain j the 144 entries edge_block[:, j, :] are distinct. Each flexibility[j] is symmetric and positive definite.
All inputs are finite; a program needn't handle non-finite values.
Results may differ from the reference program's by a relative error of at most 0.0003.
Values sent between devices are 32-bit elements; how exact they have to be, the bound alone decides.
A program may use at most 64 MiB of HBM per device.

```python
import math
import jax
import jax.numpy as jnp
from jax import lax

EDGES = 4096
SEGMENTS = 4096
PATTERNS = 128
ROUNDS = 6
SHARE_DEV = 24
ITERS = 4
SUBS = 16
ROWS = 256
N_SEG = 16


def draw_flexibility(key, part):
    key = jax.random.fold_in(key, 11)

    def per_subdomain(number):
        sub_key = jax.random.fold_in(key, number)
        first_key, second_key = jax.random.split(sub_key, 2)
        raw_values = jax.random.uniform(first_key, (EDGES, EDGES), jnp.float32, -1.0, 1.0)
        coupling = (raw_values + jnp.transpose(raw_values)) * (0.4 / math.sqrt(EDGES))
        diagonal = jax.random.uniform(second_key, (EDGES,), jnp.float32, 1.0, 2.0)
        matrix = coupling + jnp.diag(diagonal)
        return matrix
    return lax.map(per_subdomain, jnp.arange(SUBS))


def draw_partner(key, part):
    key = jax.random.fold_in(key, 23)
    label_key, round_key = jax.random.split(key)
    relabel = jax.random.permutation(label_key, SUBS).astype(jnp.int32)
    chosen = jax.random.randint(round_key, (ROUNDS,), 0, SUBS - 1).astype(jnp.int32)

    def per_round(turn):
        labels = jnp.arange(SUBS, dtype=jnp.int32)
        circle = SUBS - 1
        mates = (2 * turn - labels) % circle
        mates = jnp.where(mates == labels, SUBS - 1, mates)
        mates = jnp.where(labels == SUBS - 1, turn, mates).astype(jnp.int32)
        return jnp.zeros((SUBS,), jnp.int32).at[relabel].set(relabel[mates])
    return lax.map(per_round, chosen)


def draw_edge_block(key, part):
    key = jax.random.fold_in(key, 37)

    def per_subdomain(number):
        ordering = jax.random.permutation(jax.random.fold_in(key, number), ROWS).astype(jnp.int32)
        return ordering[:ROUNDS * SHARE_DEV].reshape(ROUNDS, SHARE_DEV)
    blocks = lax.map(per_subdomain, jnp.arange(SUBS))
    return jnp.transpose(blocks, (1, 0, 2))


def steps_of(own_key, dims, shards, least, high):
    level, own = 1.0, jax.random.fold_in(own_key, 6)
    for axis_at, parts in shards:
        draws = jnp.exp(jax.random.uniform(jax.random.fold_in(own, axis_at), (parts,), jnp.float32, least / len(shards), high / len(shards)))
        level = level * jnp.repeat(draws, dims[axis_at] // parts).reshape([-1 if axis == axis_at else 1 for axis in range(len(dims))])
    return level


def gaussian(stream_key, extent, deviation, bound, pieces=(), kind=jnp.bfloat16):
    drawn = jax.random.normal(stream_key, extent, jnp.float32) * deviation
    if len(pieces) > 0:
        drawn = steps_of(stream_key, extent, pieces, -0.22, 0.18) * drawn
    return jnp.clip(drawn, min=-bound, max=bound).astype(kind)


def setup_inputs(seed: int = 0) -> dict:
    streams_of = jax.random.split(jax.random.key(seed), 9)
    return {
        "edge_mid": jnp.clip(jax.random.uniform(streams_of[0], (SUBS, 3, EDGES), jnp.float32, -1.0, 1.0) * steps_of(streams_of[0], (SUBS, 3, EDGES), ((0, 16), (2, 16)), -0.4, 0.0), -1.0, 1.0),
        "edge_dir": gaussian(streams_of[1], (SUBS, 3, EDGES), 1.0, 6.0, ((0, 16), (2, 16)), jnp.float32),
        "seg_mid": jnp.clip(jax.random.uniform(streams_of[2], (3, SEGMENTS), jnp.float32, -1.5, 1.5) * steps_of(streams_of[2], (3, SEGMENTS), ((1, 16),), -0.4, 0.0), -1.5, 1.5),
        "seg_vec": gaussian(streams_of[3], (3, SEGMENTS), SEGMENTS ** -0.5, 0.09375, ((1, 16),), jnp.float32),
        "currents": gaussian(streams_of[4], (PATTERNS, SEGMENTS), 1.0, 6.0, ((1, 16),), jnp.float32),
        "flexibility": draw_flexibility(jax.random.fold_in(streams_of[8], 71), 0),
        "partner": draw_partner(jax.random.fold_in(streams_of[8], 71), 0),
        "edge_block": draw_edge_block(jax.random.fold_in(streams_of[8], 71), 0),
    }


core_radius = 0.05
highest = lax.Precision.HIGHEST

def source_trace(edge_mid, edge_dir, seg_mid, seg_vec, currents):

    def per_subdomain(geometry):
        midpoints, vectors = geometry
        distance = jnp.zeros((EDGES, SEGMENTS), jnp.float32)
        aligned = jnp.zeros((EDGES, SEGMENTS), jnp.float32)
        for component in range(3):
            spacing = midpoints[component][:, None] - seg_mid[component][None, :]
            distance = distance + spacing * spacing
            aligned = aligned + vectors[component][:, None] * seg_vec[component][None, :]
        kernel = aligned / jnp.sqrt(distance + core_radius * core_radius)
        return lax.dot_general(kernel, currents, (((1,), (1,)), ((), ())), precision=highest, preferred_element_type=jnp.float32)
    return lax.map(per_subdomain, (edge_mid, edge_dir))

def schur_apply(flexibility, trace_in):

    def per_subdomain(operands):
        return jnp.dot(operands[0], operands[1], precision=highest, preferred_element_type=jnp.float32)
    return lax.map(per_subdomain, (flexibility, trace_in))

def shared_index(edge_block):
    row_count = EDGES // N_SEG
    offsets = jnp.arange(N_SEG, dtype=jnp.int32) * row_count
    located = offsets[None, None, :, None] + edge_block[:, :, None, :].astype(jnp.int32)
    return jnp.transpose(located, (1, 0, 2, 3)).reshape(SUBS, ROUNDS, N_SEG * SHARE_DEV)

def jump_of(trace_in, located, partners, sign_of):
    subject = jnp.arange(SUBS, dtype=jnp.int32)[:, None, None]
    picked = trace_in[subject, located]
    opposite = picked[partners, jnp.arange(ROUNDS, dtype=jnp.int32)[None, :]]
    return sign_of[:, :, None, None] * (picked - opposite)

def spread(dual, located, sign_of):
    subject = jnp.broadcast_to(jnp.arange(SUBS, dtype=jnp.int32)[:, None, None], located.shape)
    values = sign_of[:, :, None, None] * dual
    return jnp.zeros((SUBS, EDGES, PATTERNS), jnp.float32).at[subject, located].add(values)

def inner_sum(owners, first, second):
    return lax.optimization_barrier(jnp.sum(owners[:, :, None, None] * first * second, axis=(0, 1, 2)))

def reference(edge_mid, edge_dir, seg_mid, seg_vec, currents, flexibility, partner, edge_block):
    located = shared_index(edge_block)
    partners = jnp.transpose(partner).astype(jnp.int32)
    subject = jnp.arange(SUBS, dtype=jnp.int32)[:, None]
    sign_of = jnp.where(partners > subject, 1.0, -1.0).astype(jnp.float32)
    owners = jnp.where(partners > subject, 1.0, 0.0).astype(jnp.float32)
    sources = source_trace(edge_mid, edge_dir, seg_mid, seg_vec, currents)
    base_trace = schur_apply(flexibility, sources)
    right_side = jump_of(base_trace, located, partners, sign_of)
    multipliers = jnp.zeros_like(right_side)
    residual = right_side
    direction = right_side
    carried = jnp.zeros_like(base_trace)
    norm_now = inner_sum(owners, residual, residual)
    for iteration in range(ITERS):
        image_trace = schur_apply(flexibility, spread(direction, located, sign_of))
        image_dual = jump_of(image_trace, located, partners, sign_of)
        step_size = norm_now / inner_sum(owners, direction, image_dual)
        multipliers = multipliers + step_size * direction
        residual = residual - step_size * image_dual
        carried = carried + step_size * image_trace
        if iteration + 1 < ITERS:
            norm_next = inner_sum(owners, residual, residual)
            direction = residual + norm_next / norm_now * direction
            norm_now = norm_next
    return (multipliers, base_trace - carried)
```

```python
import jax
import jax.numpy as jnp
from jax import lax
from jax.experimental import pallas as pl
from jax.experimental.pallas import tpu as pltpu
from jax.sharding import PartitionSpec as P

ITERS = 4
ROUNDS = 6
SHARE = 24
PICKS = ROUNDS * SHARE
BAND = PICKS // 2
MSG = BAND + 8
ROWS = 256
LANES = 128
HALF = LANES // 2
CHIPS = 8
MAIN = CHIPS * LANES
DEPTH = CHIPS * PICKS
CORE2 = 0.05 * 0.05
f32 = jnp.float32
bf16 = jnp.bfloat16
MESH = pl.DeviceIdType.MESH

PLANE = ((0, 1), (1, 0), (-1, 0), (1, 1), (-1, 1), (2, 0), (2, 1))
NEAR = ((0, 1), (1, 0), (-1, 0), (1, 1), (-1, 1))
FAR = (3, -3)


def split2(value):
    high = value.astype(bf16)
    return high, (value - high.astype(f32)).astype(bf16)


def dot(a, b):
    return jnp.dot(a, b, preferred_element_type=f32)


def kernel(em, ed, sm, sv, cur, part, eb, flex,
           mult_out, trace_out,
           geo, cg, sg, xg, fg,
           wa0, wa1, wa2, wa3, wb0, wb1, wb2, wb3, fw, far_s, far_r, ffs, ffr,
           fv, fhi, flo, fsh, fsl, rem, kh, kl, cb, xb, pt, pk, ptb, pb, est, ebc,
           sgn, own, base, tr, ts, tp, car, vr, vs, vp, vx,
           fsem, gsend, grecv, dsend, drecv, ssend, srecv, nsend, nrecv, zsend, zrecv):
    seg = lax.axis_index("seg")
    sub = lax.axis_index("sub")
    x, ylo, c = seg // 4, (seg // 2) % 2, seg % 2
    z, yh = sub // 2, sub % 2
    q = seg // 2
    windows = ((wa0, wa1, wa2, wa3), (wb0, wb1, wb2, wb3))

    def plane_dev(dx, fy, fc):
        yy = 1 - ylo if fy else ylo
        cc = 1 - c if fc else c
        return (((x + dx + 4) % 4) * 4 + yy * 2 + cc, sub)

    def column_dev(dz, fy):
        yy = 1 - yh if fy else yh
        return (seg, ((z + dz + 8) % 8) * 2 + yy)

    def chip_from(dx, fy):
        yy = 1 - ylo if fy else ylo
        return ((x - dx + 4) % 4) * 2 + yy

    def remote(src, dst, ss, rs, dev):
        return pltpu.make_async_remote_copy(
            src_ref=src, dst_ref=dst, send_sem=ss, recv_sem=rs, device_id=dev, device_id_type=MESH)

    pending = []
    around = [(dx, fy, fc) for dx, fy in PLANE for fc in (0, 1)] + [(0, 0, 1)]

    def low_lanes(rows):
        return lax.broadcasted_iota(jnp.int32, (rows, LANES), 1) < HALF

    def swap(value):
        return pltpu.roll(value, HALF, 1)

    flex_copy = pltpu.make_async_copy(flex.at[0], fv, fsem)
    flex_copy.start()
    barrier = pltpu.get_barrier_semaphore()
    for dx, fy, fc in around:
        pl.semaphore_signal(barrier, inc=1, device_id=plane_dev(dx, fy, fc), device_id_type=MESH)
    for dz, fy in NEAR:
        pl.semaphore_signal(barrier, inc=1, device_id=column_dev(dz, fy), device_id_type=MESH)
    for dz in FAR:
        pl.semaphore_signal(barrier, inc=1, device_id=column_dev(dz, 0), device_id_type=MESH)
    geo[c, q, 0:3, :] = sm[...]
    geo[c, q, 3:6, :] = sv[...]
    geo[c, q, 6:8, :] = jnp.zeros((2, ROWS), f32)
    turned = cur[...].T
    left = low_lanes(LANES)
    cg[0, c, q] = jnp.where(left, turned[:LANES], swap(turned[LANES:]))
    cg[1, c, q] = jnp.where(left, swap(turned[:LANES]), turned[LANES:])
    pl.semaphore_wait(barrier, len(around) + len(NEAR) + len(FAR))

    geo_copies = []
    for k, (dx, fy, fc) in enumerate(around):
        copy = remote(geo.at[c, q], geo.at[c, q], gsend.at[k], grecv.at[k], plane_dev(dx, fy, fc))
        copy.start()
        geo_copies.append(copy)
    pending.extend(geo_copies)

    def gather_start(buf, g):
        mine = buf.at[c, q]
        for k, (dx, fy) in enumerate(PLANE):
            copy = remote(mine, mine, dsend.at[g, k], drecv.at[g, k], plane_dev(dx, fy, 0))
            copy.start()
            pending.append(copy)
        k = len(PLANE)
        copy = remote(mine, mine, ssend.at[g, k], srecv.at[g, k], plane_dev(0, 0, 1))
        copy.start()
        pending.append(copy)

    def gather_near(buf, g, each):
        each(c, q)
        for k, (dx, fy) in enumerate(PLANE):
            origin = chip_from(dx, fy)
            here = buf.at[c, origin]
            remote(here, here, dsend.at[g, k], drecv.at[g, k], plane_dev(0, 0, 1)).wait_recv()
            copy = remote(here, here, ssend.at[g, k], srecv.at[g, k], plane_dev(0, 0, 1))
            copy.start()
            pending.append(copy)
            each(c, origin)

    def gather_far(buf, g, each):
        for k, (dx, fy) in ((7, (0, 0)),) + tuple(enumerate(PLANE)):
            origin = chip_from(dx, fy)
            here = buf.at[1 - c, origin]
            remote(here, here, ssend.at[g, k], srecv.at[g, k], plane_dev(0, 0, 1)).wait_recv()
            each(1 - c, origin)

    gather_start(cg.at[0], 0)
    gather_start(cg.at[1], 1)

    lane_at = lax.broadcasted_iota(jnp.int32, (1, ROWS), 1)
    pt[...] = jnp.zeros((ROWS, ROWS), f32)
    pk[...] = jnp.zeros((ROWS, ROWS), f32)

    def hot_row(k, carry):
        row = jnp.where(lane_at == eb[k // SHARE, 0, k % SHARE], 1.0, 0.0).astype(f32)
        upper = k // BAND
        at = k - upper * BAND
        place = jnp.where(at < HALF, upper * HALF + at, LANES + upper * 8 + at - HALF)
        pt[pl.ds(k, 1), :] = row
        pk[pl.ds(place, 1), :] = row
        return carry
    lax.fori_loop(0, PICKS, hot_row, 0)
    ptb[...] = pt[0:PICKS, :].astype(bf16)
    pb[...] = pk[...].T

    est[...] = jnp.zeros((LANES, ROWS), f32)
    for comp in range(3):
        est[comp:comp + 1, :] = em[comp]
        est[3 + comp:4 + comp, :] = ed[comp]
    columns = est[...].T
    for comp in range(6):
        ebc[comp] = jnp.broadcast_to(columns[:, comp:comp + 1], (ROWS, LANES))

    left_band = low_lanes(SHARE)
    for b in range(3):
        band = slice(b * SHARE, (b + 1) * SHARE)
        first = jnp.where(part[b, sub] > sub, 1.0, 0.0).astype(f32)
        second = jnp.where(part[b + 3, sub] > sub, 1.0, 0.0).astype(f32)
        mark = jnp.where(left_band, first, second)
        own[band, :] = mark
        sgn[band, :] = mark * 2.0 - 1.0

    for k, (dx, fy, fc) in enumerate(around):
        geo_copies[k].wait_recv()

    def tile(step, carry):
        half, chip = step // CHIPS, step % CHIPS
        for h in range(2):
            row = [geo[half, chip, pl.ds(comp, 1), h * LANES:(h + 1) * LANES] for comp in range(6)]
            lanes = pl.ds(pl.multiple_of(chip * ROWS + h * LANES, LANES), LANES)
            for part_at in range(4):
                rows = slice(part_at * 64, part_at * 64 + 64)
                dist = jnp.full((64, LANES), CORE2, f32)
                along = jnp.zeros((64, LANES), f32)
                for comp in range(3):
                    gap = ebc[comp, rows, :] - row[comp]
                    dist = dist + gap * gap
                    along = along + ebc[3 + comp, rows, :] * row[3 + comp]
                high, low = split2(along * lax.rsqrt(dist))
                kh[half, rows, lanes] = high
                kl[half, rows, lanes] = low
        return carry
    lax.fori_loop(0, 2 * CHIPS, tile, 0)

    def unpack(value):
        high = value.astype(bf16).astype(f32)
        low = value - high
        side = low_lanes(value.shape[0])
        return jnp.where(side, high, swap(low)), jnp.where(side, swap(high), low)

    def dense_block(buf, h):
        def each(half, chip):
            one, two = unpack(buf[half, chip])
            cb[h, half, pl.ds(pl.multiple_of(chip * ROWS, LANES), LANES), :] = one.astype(bf16)
            cb[h, half, pl.ds(pl.multiple_of(chip * ROWS + LANES, LANES), LANES), :] = two.astype(bf16)
        return each

    def dense_dot(high, low, half, h):
        return dot(high[half], cb[h, half]) + dot(low[half], cb[h, half])

    def split_flex(step, carry):
        half, chip = step // CHIPS, step % CHIPS
        for h in range(2):
            src = pl.ds(pl.multiple_of((chip * 2 + half) * ROWS + h * LANES, LANES), LANES)
            dst = pl.ds(pl.multiple_of(chip * ROWS + h * LANES, LANES), LANES)
            high, low = split2(fv[:, src])
            fhi[half, :, dst] = high
            flo[half, :, dst] = low
        return carry

    def pick_columns(half):
        rem[...] = jnp.zeros((2, ROWS, LANES), f32)

        def one(chip, carry):
            tail = pltpu.roll(pb[:, LANES:], chip * (PICKS - LANES), 1)
            choose = jnp.concatenate([pb[:, :LANES], tail], axis=1).astype(bf16)
            src = pl.ds(pl.multiple_of(chip * ROWS, ROWS), ROWS)
            dst = pl.ds(pl.multiple_of(chip * LANES, LANES), LANES)
            for at, (whole, out) in enumerate(((fhi, fsh), (flo, fsl))):
                got = dot(whole[half, :, src], choose)
                out[half, :, dst] = got[:, :LANES].astype(bf16)
                rem[at] += got[:, LANES:]
            return carry
        lax.fori_loop(0, CHIPS, one, 0)
        fsh[half, :, MAIN:] = rem[0].astype(bf16)
        fsl[half, :, MAIN:] = rem[1].astype(bf16)

    def pick_rows(full):
        high = full.astype(bf16)
        rest = full - high.astype(f32)
        mid = rest.astype(bf16)
        low = (rest - mid.astype(f32)).astype(bf16)
        both = dot(ptb[...], jnp.where(low_lanes(ROWS), high.astype(f32), mid.astype(f32)).astype(bf16))
        picked = (both + swap(both)) + dot(ptb[...], low)
        return jnp.where(low_lanes(BAND), picked[:BAND], picked[BAND:])

    def near_slot(dz, fy):
        return (dz + 1) * 2 + fy

    def near_start(buf, e):
        mine = buf.at[near_slot(0, 0)]
        for k, (dz, fy) in enumerate(NEAR):
            copy = remote(mine, buf.at[near_slot(-dz, fy)], nsend.at[e, k], nrecv.at[e, k], column_dev(dz, fy))
            copy.start()
            pending.append(copy)

    def near_wait(buf, e):
        for k, (dz, fy) in enumerate(NEAR):
            here = buf.at[near_slot(-dz, fy)]
            remote(here, here, nsend.at[e, k], nrecv.at[e, k], column_dev(dz, fy)).wait_recv()

    def far_start(src, dst, e):
        for t, dz in enumerate(FAR):
            copy = remote(src.at[t], dst.at[t], zsend.at[e, t], zrecv.at[e, t], column_dev(dz, 0))
            copy.start()
            pending.append(copy)

    def far_wait(dst, e):
        for t, dz in enumerate(FAR):
            here = dst.at[t]
            remote(here, here, zsend.at[e, t], zrecv.at[e, t], column_dev(dz, 0)).wait_recv()

    def place_of(r, at):
        p = part[r, at]
        rel = (p // 2 - z + 8) % 8
        shifted = (rel + 1) % 8
        slot = shifted * 2 + jnp.where(p % 2 == yh, 0, 1)
        inside = shifted < 3
        return rel, inside, jnp.where(inside, slot, 0)

    far_places = [[place_of(r, ((z + dz + 8) % 8) * 2 + yh)[2] for r in range(ROUNDS)] for dz in FAR]
    my_places = [place_of(r, sub) for r in range(ROUNDS)]

    def sums_far(buf, dst, at):
        keep = [buf[s, at:at + 8, :] for s in range(6)]
        upper = (keep[2] + keep[3]) + (keep[4] + keep[5])
        whole = upper + (keep[0] + keep[1])
        dst[0, at:at + 8, :] = upper
        dst[1, at:at + 8, :] = whole
        return whole

    def sparse_block(buf, h):
        def each(half, chip):
            one, two = unpack(buf[half, chip, 0:BAND, :])
            for at, value in ((0, one), (HALF, two)):
                rows = pl.ds(pl.multiple_of(chip * LANES + at, HALF), HALF)
                xb[h, half, rows, :] = value[:HALF].astype(bf16)
            tail = pl.ds(pl.multiple_of(MAIN + chip * 16, 16), 16)
            xb[h, half, tail, :] = jnp.concatenate([one[HALF:], two[HALF:]], axis=0).astype(bf16)
        return each

    def sparse_dot(half, h):
        return dot(fsh[half], xb[h, half]) + dot(fsl[half], xb[h, half])

    zeros8 = jnp.zeros((8, LANES), f32)

    def inner_rows(residual, image):
        gamma = jnp.sum(own[...] * residual * residual, axis=0, keepdims=True)
        delta = jnp.sum(residual * image, axis=0, keepdims=True)
        return jnp.concatenate([gamma, delta, jnp.zeros((6, LANES), f32)], axis=0)

    def chain(h):
        cur_block, src_block = dense_block(cg.at[h], h), dense_block(sg.at[h], h)
        gather_near(cg.at[h], h, cur_block)
        yield
        total = dense_dot(kh, kl, c, h)
        gather_far(cg.at[h], h, cur_block)
        total = total + dense_dot(kh, kl, 1 - c, h)
        total = total + swap(total)
        sg[h, c, q] = jnp.where(left, total[:LANES], total[LANES:])
        gather_start(sg.at[h], 2 + h)
        yield
        gather_near(sg.at[h], 2 + h, src_block)
        yield
        total = dense_dot(fhi, flo, c, h)
        gather_far(sg.at[h], 2 + h, src_block)
        total = total + dense_dot(fhi, flo, 1 - c, h)
        total = total + swap(total)
        base[h] = total
        mine = pick_rows(total)
        scalars = zeros8
        gamma_was = alpha_was = None
        for g in range(ITERS + 1):
            e = g * 2 + h
            buf = windows[h][g] if g < ITERS else fw.at[h]
            if g == ITERS:
                buf[near_slot(0, 0)] = scalars
                near_start(buf, e)
                yield
                near_wait(buf, e)
                whole = sums_far(buf, ffs.at[h], 0)
                far_start(ffs.at[h], ffr.at[h], e)
                yield
                far_wait(ffr.at[h], e)
                fg[h, c, q] = whole + ffr[h, 0] + ffr[h, 1]
                gather_start(fg.at[h], 12 + h)
                yield
                gather_near(fg.at[h], 12 + h, lambda half, chip: None)
                yield
                gather_far(fg.at[h], 12 + h, lambda half, chip: None)
                sums = zeros8
                for half in range(2):
                    for chip in range(CHIPS):
                        sums = sums + fg[h, half, chip]
            else:
                buf[near_slot(0, 0), 0:BAND, :] = mine
                buf[near_slot(0, 0), BAND:MSG, :] = scalars
                near_start(buf, e)
                yield
                near_wait(buf, e)
                for t in range(2):
                    for b in range(3):
                        band = slice(b * SHARE, (b + 1) * SHARE)
                        far_s[e, t, band, :] = jnp.where(
                            left_band, buf[far_places[t][b], band, :], buf[far_places[t][b + 3], band, :])
                whole = sums_far(buf, far_s.at[e], BAND)
                far_start(far_s.at[e], far_r.at[e], e)
                yield
                far_wait(far_r.at[e], e)
                pieces = []
                for b in range(3):
                    band = slice(b * SHARE, (b + 1) * SHARE)
                    sides = []
                    for r in (b, b + 3):
                        rel, inside, slot = my_places[r]
                        away = jnp.where(rel < 5, far_r[e, 1, band, :], far_r[e, 0, band, :])
                        sides.append(jnp.where(inside, buf[slot, band, :], away))
                    pieces.append(mine[band, :] - jnp.where(left_band, sides[0], sides[1]))
                vector = jnp.concatenate(pieces, axis=0)
                xg[e, c, q, 0:BAND, :] = vector
                xg[e, c, q, BAND:MSG, :] = whole + far_r[e, 0, BAND:MSG, :] + far_r[e, 1, BAND:MSG, :]
                gather_start(xg.at[e], 4 + e)
                yield
                block = sparse_block(xg.at[e], h)
                gather_near(xg.at[e], 4 + e, block)
                yield
                total = sparse_dot(c, h)
                gather_far(xg.at[e], 4 + e, block)
                total = total + sparse_dot(1 - c, h)
                applied = total + swap(total)
                sums = zeros8
                for half in range(2):
                    for chip in range(CHIPS):
                        sums = sums + xg[e, half, chip, BAND:MSG, :]
            if g == 0:
                vr[h] = vector
                tr[h] = applied
                mine = pick_rows(applied)
                scalars = inner_rows(vector, mine)
                continue
            sums = sums + swap(sums)
            gamma, delta = sums[0:1], sums[1:2]
            residual = vr[h]
            if g == 1:
                alpha = gamma / delta
                step, direction = vector, residual
                step_image = applied
            else:
                beta = gamma / gamma_was
                alpha = gamma / (delta - beta * gamma / alpha_was)
                direction = residual + beta * vp[h]
                if g < ITERS:
                    step = vector + beta * vs[h]
                    step_image = applied + beta * ts[h]
            if g < ITERS:
                image = tr[h]
                fresh = image - alpha * step_image
                mine = pick_rows(fresh)
                residual = residual - alpha * step
                scalars = inner_rows(residual, mine)
                direction_image = image if g == 1 else image + beta * tp[h]
                vr[h] = residual
                vs[h] = step
                ts[h] = step_image
                tr[h] = fresh
                vp[h] = direction
                tp[h] = direction_image
                if g == 1:
                    vx[h] = alpha * direction
                    car[h] = alpha * direction_image
                else:
                    vx[h] += alpha * direction
                    car[h] += alpha * direction_image
            else:
                vx[h] += alpha * direction
                car[h] += alpha * (tr[h] + beta * tp[h])
            gamma_was, alpha_was = gamma, alpha

    chains = (chain(0), chain(1))

    def go(which):
        next(chains[which], None)

    go(0)
    go(0)
    go(1)
    go(1)
    flex_copy.wait()
    lax.fori_loop(0, 2 * CHIPS, split_flex, 0)
    go(0)
    go(0)
    go(1)
    go(1)
    go(0)
    pick_columns(0)
    go(1)
    pick_columns(1)
    go(0)
    go(1)
    go(0)
    go(0)
    go(1)
    go(1)
    for _ in range(ITERS):
        for which in (0, 1, 0, 1, 0, 0, 1, 1):
            go(which)

    side = low_lanes(ROWS)
    trace_out[0] = jnp.where(side, base[0] - car[0], base[1] - car[1])
    for b in range(3):
        band = slice(b * SHARE, (b + 1) * SHARE)
        lower, upper = vx[0, band, :], vx[1, band, :]
        sign = sgn[band, :]
        lower, upper = sign * lower, sign * upper
        mult_out[0, b] = jnp.where(left_band, lower, swap(upper))
        mult_out[0, b + 3] = jnp.where(left_band, swap(lower), upper)

    for copy in pending:
        copy.wait_send()


def body(edge_mid, edge_dir, seg_mid, seg_vec, currents, flexibility, partner, edge_block):
    vmem = pl.BlockSpec(memory_space=pltpu.VMEM)
    smem = pl.BlockSpec(memory_space=pltpu.SMEM)
    dma = pltpu.SemaphoreType.DMA
    half = CHIPS * ROWS

    def room(*shape):
        return pltpu.VMEM(shape, f32)

    def short(*shape):
        return pltpu.VMEM(shape, bf16)
    both = 2 * ITERS
    scratch = [
        room(2, CHIPS, 8, ROWS),
        room(2, 2, CHIPS, LANES, LANES),
        room(2, 2, CHIPS, LANES, LANES),
        room(both, 2, CHIPS, MSG, LANES),
        room(2, 2, CHIPS, 8, LANES),
    ]
    scratch += [room(6, MSG, LANES)] * both
    scratch += [room(2, 6, 8, LANES), room(both, 2, MSG, LANES), room(both, 2, MSG, LANES)]
    scratch += [room(2, 2, 8, LANES), room(2, 2, 8, LANES)]
    scratch += [
        room(ROWS, 2 * half), short(2, ROWS, half), short(2, ROWS, half),
        short(2, ROWS, DEPTH), short(2, ROWS, DEPTH), room(2, ROWS, LANES),
        short(2, ROWS, half), short(2, ROWS, half),
        short(2, 2, half, LANES), short(2, 2, DEPTH, LANES),
        room(ROWS, ROWS), room(ROWS, ROWS), short(PICKS, ROWS), room(ROWS, ROWS),
        room(LANES, ROWS), room(6, ROWS, LANES),
        room(BAND, LANES), room(BAND, LANES),
    ]
    scratch += [room(2, ROWS, LANES)] * 5
    scratch += [room(2, BAND, LANES)] * 4
    scratch += [
        dma, dma((15,)), dma((15,)),
        dma((14, 7)), dma((14, 7)), dma((14, 8)), dma((14, 8)),
        dma((10, 5)), dma((10, 5)), dma((10, 2)), dma((10, 2)),
    ]
    return pl.pallas_call(
        kernel,
        out_shape=(
            jax.ShapeDtypeStruct((1, ROUNDS, SHARE, LANES), f32),
            jax.ShapeDtypeStruct((1, ROWS, LANES), f32),
        ),
        in_specs=[vmem] * 5 + [smem] * 2 + [pl.BlockSpec(memory_space=pl.ANY)],
        out_specs=(vmem, vmem),
        scratch_shapes=scratch,
        compiler_params=pltpu.CompilerParams(
            collective_id=0, has_side_effects=True, vmem_limit_bytes=56 * 1024 * 1024),
        name="interface_cg",
    )(jnp.transpose(edge_mid, (1, 0, 2)), jnp.transpose(edge_dir, (1, 0, 2)),
      seg_mid, seg_vec, currents, partner, edge_block, flexibility)


def solution(mesh):
    in_specs = (
        P("sub", None, "seg"),
        P("sub", None, "seg"),
        P(None, "seg"),
        P(None, "seg"),
        P(None, "seg"),
        P("sub", "seg", None),
        P(),
        P(None, "sub", None),
    )
    out_specs = (P("sub", None, "seg", None), P("sub", "seg", None))
    return jax.shard_map(body, mesh=mesh, in_specs=in_specs, out_specs=out_specs, check_vma=False)
```

```python
import jax
import jax.numpy as jnp
from jax import lax
from jax.experimental import pallas as pl
from jax.experimental.pallas import tpu as pltpu
from jax.sharding import PartitionSpec as P

ITERS = 4
ROUNDS = 6
SHARE = 24
PICKS = ROUNDS * SHARE
BAND = PICKS // 2
MSG = BAND + 8
ROWS = 256
LANES = 128
HALF = LANES // 2
CHIPS = 8
MAIN = CHIPS * LANES
DEPTH = CHIPS * PICKS
CORE2 = 0.05 * 0.05
f32 = jnp.float32
bf16 = jnp.bfloat16
MESH = pl.DeviceIdType.MESH

PLANE = ((0, 1), (1, 0), (-1, 0), (1, 1), (-1, 1), (2, 0), (2, 1))
NEAR = ((0, 1), (1, 0), (-1, 0), (1, 1), (-1, 1))
FAR = (3, -3)
COLUMN = tuple((dz, fy) for dz in (4, -3, 3, -2, 2, -1, 1, 0) for fy in (1, 0) if dz or fy)


def split2(value):
    high = value.astype(bf16)
    return high, (value - high.astype(f32)).astype(bf16)


def dot(a, b):
    return jnp.dot(a, b, preferred_element_type=f32)


def kernel(em, ed, sm, sv, cur, part, eb, flex,
           mult_out, trace_out,
           geo, ge, cg, sg, xg, fg, ps, pr, pps, ppr, fps, fpr,
           wa0, wa1, wa2, wa3, wb0, wb1, wb2, wb3, fw, far_s, far_r,
           fv, fhi, flo, fsh, fsl, fssh, fssl, rem, kh, kl, cb, xb, pt, pk, ptb, pb, est, ebc,
           sgn, own, base, tx, tr, tp, trp, tsp, vr, vs, vp, vx,
           fsem, fsend, frecv, esend, erecv, gsend, grecv, dsend, drecv, psend, precv,
           nsend, nrecv, zsend, zrecv, asend, arecv):
    seg = lax.axis_index("seg")
    sub = lax.axis_index("sub")
    x, ylo, c = seg // 4, (seg // 2) % 2, seg % 2
    z, yh = sub // 2, sub % 2
    q = seg // 2
    windows = ((wa0, wa1, wa2, wa3), (wb0, wb1, wb2, wb3))

    def plane_dev(dx, fy, fc):
        yy = 1 - ylo if fy else ylo
        cc = 1 - c if fc else c
        return (((x + dx + 4) % 4) * 4 + yy * 2 + cc, sub)

    def column_dev(dz, fy):
        yy = 1 - yh if fy else yh
        return (seg, ((z + dz + 8) % 8) * 2 + yy)

    def chip_from(dx, fy):
        yy = 1 - ylo if fy else ylo
        return ((x - dx + 4) % 4) * 2 + yy

    def remote(src, dst, ss, rs, dev):
        return pltpu.make_async_remote_copy(
            src_ref=src, dst_ref=dst, send_sem=ss, recv_sem=rs, device_id=dev, device_id_type=MESH)

    pending = []
    sibling = plane_dev(0, 0, 1)

    def low_lanes(rows):
        return lax.broadcasted_iota(jnp.int32, (rows, LANES), 1) < HALF

    def swap(value):
        return pltpu.roll(value, HALF, 1)

    flex_copies = []
    for chip in range(CHIPS):
        src = flex.at[0, :, pl.ds(pl.multiple_of((chip * 2 + c) * ROWS, ROWS), ROWS)]
        copy = pltpu.make_async_copy(src, fv.at[c, :, chip * ROWS:(chip + 1) * ROWS], fsem.at[chip])
        copy.start()
        flex_copies.append(copy)
    barrier = pltpu.get_barrier_semaphore()
    peers = [plane_dev(dx, fy, 0) for dx, fy in PLANE] + [sibling]
    peers += [column_dev(dz, fy) for dz, fy in COLUMN]
    for peer in peers:
        pl.semaphore_signal(barrier, inc=1, device_id=peer, device_id_type=MESH)
    geo[q, 0:3, :] = sm[...]
    geo[q, 3:6, :] = sv[...]
    geo[q, 6:8, :] = jnp.zeros((2, ROWS), f32)
    for comp in range(3):
        ge[c, comp:comp + 1, :] = em[comp]
        ge[c, 3 + comp:4 + comp, :] = ed[comp]
    ge[c, 6:8, :] = jnp.zeros((2, ROWS), f32)
    turned = cur[...].T
    left = low_lanes(LANES)
    cg[0, q] = jnp.where(left, turned[:LANES], swap(turned[LANES:]))
    cg[1, q] = jnp.where(left, swap(turned[:LANES]), turned[LANES:])
    pl.semaphore_wait(barrier, len(peers))

    edge_copy = remote(ge.at[c], ge.at[c], esend, erecv, sibling)
    edge_copy.start()
    pending.append(edge_copy)
    geo_copies = []
    for k, (dx, fy) in enumerate(PLANE):
        copy = remote(geo.at[q], geo.at[q], gsend.at[k], grecv.at[k], plane_dev(dx, fy, 0))
        copy.start()
        geo_copies.append(copy)
    pending.extend(geo_copies)

    def gather_start(buf, g):
        mine = buf.at[q]
        for k, (dx, fy) in enumerate(PLANE):
            copy = remote(mine, mine, dsend.at[g, k], drecv.at[g, k], plane_dev(dx, fy, 0))
            copy.start()
            pending.append(copy)

    def gather_wait(buf, g, each):
        each(q)
        for k, (dx, fy) in enumerate(PLANE):
            origin = chip_from(dx, fy)
            here = buf.at[origin]
            remote(here, here, dsend.at[g, k], drecv.at[g, k], sibling).wait_recv()
            each(origin)

    gather_start(cg.at[0], 0)
    gather_start(cg.at[1], 1)
    shared_copies = []
    for chip in range(CHIPS):
        src = flex.at[0, :, pl.ds(pl.multiple_of((chip * 2 + 1 - c) * ROWS, ROWS), ROWS)]
        dst = fv.at[c, :, chip * ROWS:(chip + 1) * ROWS]
        copy = remote(src, dst, fsend.at[chip], frecv.at[chip], sibling)
        copy.start()
        shared_copies.append(copy)
    pending.extend(shared_copies)

    lane_at = lax.broadcasted_iota(jnp.int32, (1, ROWS), 1)
    pt[...] = jnp.zeros((ROWS, ROWS), f32)
    pk[...] = jnp.zeros((ROWS, ROWS), f32)

    def hot_row(k, carry):
        row = jnp.where(lane_at == eb[k // SHARE, 0, k % SHARE], 1.0, 0.0).astype(f32)
        upper = k // BAND
        at = k - upper * BAND
        place = jnp.where(at < HALF, upper * HALF + at, LANES + upper * 8 + at - HALF)
        pt[pl.ds(k, 1), :] = row
        pk[pl.ds(place, 1), :] = row
        return carry
    lax.fori_loop(0, PICKS, hot_row, 0)
    ptb[...] = pt[0:PICKS, :].astype(bf16)
    pb[...] = pk[...].T

    edge_copy.wait_recv()
    for side in range(2):
        est[...] = jnp.zeros((LANES, ROWS), f32)
        est[0:8, :] = ge[side]
        columns = est[...].T
        for comp in range(6):
            ebc[side, comp] = jnp.broadcast_to(columns[:, comp:comp + 1], (ROWS, LANES))

    left_band = low_lanes(SHARE)
    for b in range(3):
        band = slice(b * SHARE, (b + 1) * SHARE)
        first = jnp.where(part[b, sub] > sub, 1.0, 0.0).astype(f32)
        second = jnp.where(part[b + 3, sub] > sub, 1.0, 0.0).astype(f32)
        mark = jnp.where(left_band, first, second)
        own[band, :] = mark
        sgn[band, :] = mark * 2.0 - 1.0

    for copy in geo_copies:
        copy.wait_recv()

    def tile(step, carry):
        side, chip = step // CHIPS, step % CHIPS
        for h in range(2):
            row = [geo[chip, pl.ds(comp, 1), h * LANES:(h + 1) * LANES] for comp in range(6)]
            lanes = pl.ds(pl.multiple_of(chip * ROWS + h * LANES, LANES), LANES)
            for part_at in range(4):
                rows = slice(part_at * 64, part_at * 64 + 64)
                dist = jnp.full((64, LANES), CORE2, f32)
                along = jnp.zeros((64, LANES), f32)
                for comp in range(3):
                    gap = ebc[side, comp, rows, :] - row[comp]
                    dist = dist + gap * gap
                    along = along + ebc[side, 3 + comp, rows, :] * row[3 + comp]
                high, low = split2(along * lax.rsqrt(dist))
                kh[side, rows, lanes] = high
                kl[side, rows, lanes] = low
        return carry
    lax.fori_loop(0, 2 * CHIPS, tile, 0)

    def unpack(value):
        high = value.astype(bf16).astype(f32)
        low = value - high
        side = low_lanes(value.shape[0])
        return jnp.where(side, high, swap(low)), jnp.where(side, swap(high), low)

    def dense_block(buf, h):
        def each(chip):
            one, two = unpack(buf[chip])
            cb[h, pl.ds(pl.multiple_of(chip * ROWS, LANES), LANES), :] = one.astype(bf16)
            cb[h, pl.ds(pl.multiple_of(chip * ROWS + LANES, LANES), LANES), :] = two.astype(bf16)
        return each

    def dense_dot(high, low, h):
        def rows_of(side):
            return dot(high[side], cb[h]) + dot(low[side], cb[h])
        return rows_of

    def combine(inst, rows_of, scalars):
        other = rows_of(1 - c)
        other = other + swap(other)
        ps[inst, 0:LANES, :] = jnp.where(left, other[:LANES], other[LANES:])
        ps[inst, LANES:LANES + 8, :] = scalars
        copy = remote(ps.at[inst], pr.at[inst], psend.at[inst], precv.at[inst], sibling)
        copy.start()
        pending.append(copy)
        mine = rows_of(c)
        mine = mine + swap(mine)
        copy.wait_recv()
        got = pr[inst, 0:LANES, :]
        back = swap(got)
        top = mine[:LANES] + jnp.where(left, got, back)
        bottom = mine[LANES:] + jnp.where(left, back, got)
        return jnp.concatenate([top, bottom], axis=0), scalars + pr[inst, LANES:LANES + 8, :]

    def split_flex(step, carry):
        side, chip = step // CHIPS, step % CHIPS
        for h in range(2):
            lanes = pl.ds(pl.multiple_of(chip * ROWS + h * LANES, LANES), LANES)
            high, low = split2(fv[side, :, lanes])
            fhi[side, :, lanes] = high
            flo[side, :, lanes] = low
        return carry

    def pick_columns(half):
        rem[...] = jnp.zeros((2, ROWS, LANES), f32)

        def one(chip, carry):
            tail = pltpu.roll(pb[:, LANES:], chip * (PICKS - LANES), 1)
            choose = jnp.concatenate([pb[:, :LANES], tail], axis=1).astype(bf16)
            src = pl.ds(pl.multiple_of(chip * ROWS, ROWS), ROWS)
            dst = pl.ds(pl.multiple_of(chip * LANES, LANES), LANES)
            for at, (whole, out) in enumerate(((fhi, fsh), (flo, fsl))):
                got = dot(whole[half, :, src], choose)
                out[half, :, dst] = got[:, :LANES].astype(bf16)
                rem[at] += got[:, LANES:]
            return carry
        lax.fori_loop(0, CHIPS, one, 0)
        fsh[half, :, MAIN:] = rem[0].astype(bf16)
        fsl[half, :, MAIN:] = rem[1].astype(bf16)
        fssh[half] = dot(ptb[...], fsh[half]).astype(bf16)
        fssl[half] = dot(ptb[...], fsl[half]).astype(bf16)

    def pick_rows(full):
        high = full.astype(bf16)
        rest = full - high.astype(f32)
        mid = rest.astype(bf16)
        low = (rest - mid.astype(f32)).astype(bf16)
        both = dot(ptb[...], jnp.where(low_lanes(ROWS), high.astype(f32), mid.astype(f32)).astype(bf16))
        picked = (both + swap(both)) + dot(ptb[...], low)
        return jnp.where(low_lanes(BAND), picked[:BAND], picked[BAND:])

    def near_slot(dz, fy):
        return (dz + 1) * 2 + fy

    def near_start(buf, e):
        mine = buf.at[near_slot(0, 0)]
        for k, (dz, fy) in enumerate(NEAR):
            copy = remote(mine, buf.at[near_slot(-dz, fy)], nsend.at[e, k], nrecv.at[e, k], column_dev(dz, fy))
            copy.start()
            pending.append(copy)

    def near_wait(buf, e):
        for k, (dz, fy) in enumerate(NEAR):
            here = buf.at[near_slot(-dz, fy)]
            remote(here, here, nsend.at[e, k], nrecv.at[e, k], column_dev(dz, fy)).wait_recv()

    def far_start(src, dst, e):
        for t, dz in enumerate(FAR):
            copy = remote(src.at[t], dst.at[t], zsend.at[e, t], zrecv.at[e, t], column_dev(dz, 0))
            copy.start()
            pending.append(copy)

    def far_wait(dst, e):
        for t, dz in enumerate(FAR):
            here = dst.at[t]
            remote(here, here, zsend.at[e, t], zrecv.at[e, t], column_dev(dz, 0)).wait_recv()

    def place_of(r, at):
        p = part[r, at]
        rel = (p // 2 - z + 8) % 8
        shifted = (rel + 1) % 8
        slot = shifted * 2 + jnp.where(p % 2 == yh, 0, 1)
        inside = shifted < 3
        return rel, inside, jnp.where(inside, slot, 0)

    far_places = [[place_of(r, ((z + dz + 8) % 8) * 2 + yh)[2] for r in range(ROUNDS)] for dz in FAR]
    my_places = [place_of(r, sub) for r in range(ROUNDS)]

    def sums_far(buf, dst, at):
        keep = [buf[s, at:at + 8, :] for s in range(6)]
        upper = (keep[2] + keep[3]) + (keep[4] + keep[5])
        whole = upper + (keep[0] + keep[1])
        dst[0, at:at + 8, :] = upper
        dst[1, at:at + 8, :] = whole
        return whole

    def sparse_write(packed, chip, h):
        one, two = unpack(packed)
        for at, value in ((0, one), (HALF, two)):
            rows = pl.ds(pl.multiple_of(chip * LANES + at, HALF), HALF)
            xb[h, rows, :] = value[:HALF].astype(bf16)
        tail = pl.ds(pl.multiple_of(MAIN + chip * 16, 16), 16)
        xb[h, tail, :] = jnp.concatenate([one[HALF:], two[HALF:]], axis=0).astype(bf16)

    def sparse_block(buf, h):
        def each(chip):
            sparse_write(buf[chip, 0:BAND, :], chip, h)
        return each

    def sparse_dot(h):
        def rows_of(side):
            return dot(fsh[side], xb[h]) + dot(fsl[side], xb[h])
        return rows_of

    def combine_picks(inst, h, scalars):
        left_pack = low_lanes(BAND)

        def rows_of(side):
            got = dot(fssh[side], xb[h]) + dot(fssl[side], xb[h])
            got = got + swap(got)
            return jnp.where(left_pack, got[:BAND], got[BAND:])
        pps[inst, 0:BAND, :] = rows_of(1 - c)
        pps[inst, BAND:MSG, :] = scalars
        copy = remote(pps.at[inst], ppr.at[inst], psend.at[inst], precv.at[inst], sibling)
        copy.start()
        pending.append(copy)
        mine = rows_of(c)
        copy.wait_recv()
        return mine + ppr[inst, 0:BAND, :], scalars + ppr[inst, BAND:MSG, :]

    def add(first, second, scale):
        out = dict(first)
        for key, value in second.items():
            out[key] = out[key] + scale * value if key in out else scale * value
        return out

    def full_rows(inst, h, weights):
        for chip in range(CHIPS):
            value = None
            for g, weight in weights.items():
                term = weight * xg[g * 2 + h, chip, 0:BAND, :]
                value = term if value is None else value + term
            sparse_write(value, chip, h)
        return combine(inst, sparse_dot(h), zeros8)[0]

    zeros8 = jnp.zeros((8, LANES), f32)

    def inner_rows(residual, image):
        gamma = jnp.sum(own[...] * residual * residual, axis=0, keepdims=True)
        delta = jnp.sum(residual * image, axis=0, keepdims=True)
        return jnp.concatenate([gamma, delta, jnp.zeros((6, LANES), f32)], axis=0)

    def chain(h):
        gather_wait(cg.at[h], h, dense_block(cg.at[h], h))
        yield
        total, _ = combine(h, dense_dot(kh, kl, h), zeros8)
        sg[h, q] = jnp.where(left, total[:LANES], total[LANES:])
        gather_start(sg.at[h], 2 + h)
        yield
        gather_wait(sg.at[h], 2 + h, dense_block(sg.at[h], h))
        yield
        total, _ = combine(2 + h, dense_dot(fhi, flo, h), zeros8)
        base[h] = total
        mine = pick_rows(total)
        scalars = zeros8
        gamma_was = alpha_was = None
        for g in range(ITERS + 1):
            e = g * 2 + h
            if g == ITERS:
                fw[h, len(COLUMN)] = scalars
                for k, (dz, fy) in enumerate(COLUMN):
                    copy = remote(fw.at[h, len(COLUMN)], fw.at[h, k], asend.at[h, k], arecv.at[h, k], column_dev(dz, fy))
                    copy.start()
                    pending.append(copy)
                yield
                tx[h] = full_rows(12 + 3 * h, h, wx)
                tr[h] = full_rows(13 + 3 * h, h, wr)
                tp[h] = full_rows(14 + 3 * h, h, wp)
                yield
                sums = scalars
                for k, (dz, fy) in enumerate(COLUMN):
                    here = fw.at[h, k]
                    remote(here, here, asend.at[h, k], arecv.at[h, k], column_dev(dz, fy)).wait_recv()
                    sums = sums + fw[h, k]
                fg[h, q] = sums
                gather_start(fg.at[h], 12 + h)
                yield
                gather_wait(fg.at[h], 12 + h, lambda chip: None)
                sums = zeros8
                for chip in range(CHIPS):
                    sums = sums + fg[h, chip]
                fps[h] = sums
                copy = remote(fps.at[h], fpr.at[h], psend.at[18 + h], precv.at[18 + h], sibling)
                copy.start()
                pending.append(copy)
                yield
                copy.wait_recv()
                sums = sums + fpr[h]
            else:
                buf = windows[h][g]
                buf[near_slot(0, 0), 0:BAND, :] = mine
                buf[near_slot(0, 0), BAND:MSG, :] = scalars
                near_start(buf, e)
                yield
                near_wait(buf, e)
                for t in range(2):
                    for b in range(3):
                        band = slice(b * SHARE, (b + 1) * SHARE)
                        far_s[e, t, band, :] = jnp.where(
                            left_band, buf[far_places[t][b], band, :], buf[far_places[t][b + 3], band, :])
                whole = sums_far(buf, far_s.at[e], BAND)
                far_start(far_s.at[e], far_r.at[e], e)
                yield
                far_wait(far_r.at[e], e)
                pieces = []
                for b in range(3):
                    band = slice(b * SHARE, (b + 1) * SHARE)
                    sides = []
                    for r in (b, b + 3):
                        rel, inside, slot = my_places[r]
                        away = jnp.where(rel < 5, far_r[e, 1, band, :], far_r[e, 0, band, :])
                        sides.append(jnp.where(inside, buf[slot, band, :], away))
                    pieces.append(mine[band, :] - jnp.where(left_band, sides[0], sides[1]))
                vector = jnp.concatenate(pieces, axis=0)
                xg[e, q, 0:BAND, :] = vector
                xg[e, q, BAND:MSG, :] = whole + far_r[e, 0, BAND:MSG, :] + far_r[e, 1, BAND:MSG, :]
                gather_start(xg.at[e], 4 + e)
                yield
                gather_wait(xg.at[e], 4 + e, sparse_block(xg.at[e], h))
                yield
                sums = zeros8
                for chip in range(CHIPS):
                    sums = sums + xg[e, chip, BAND:MSG, :]
                applied, sums = combine_picks(4 + e, h, sums)
            if g == 0:
                vr[h] = vector
                trp[h] = applied
                mine = applied
                scalars = inner_rows(vector, mine)
                wr = {0: jnp.ones((1, LANES), f32)}
                continue
            sums = sums + swap(sums)
            gamma, delta = sums[0:1], sums[1:2]
            residual = vr[h]
            if g == 1:
                alpha = gamma / delta
                step, direction, step_image = vector, residual, applied
                wp, ws = wr, {}
            else:
                beta = gamma / gamma_was
                alpha = gamma / (delta - beta * gamma / alpha_was)
                direction = residual + beta * vp[h]
                if g < ITERS:
                    step = vector + beta * vs[h]
                    step_image = applied + beta * tsp[h]
                    wp = add(wr, wp, beta)
                    ws = add({}, ws, beta)
            if g < ITERS:
                mine = trp[h] - alpha * step_image
                residual = residual - alpha * step
                scalars = inner_rows(residual, mine)
                ws[g] = jnp.ones((1, LANES), f32)
                wx = add(wx if g > 1 else {}, wp, alpha)
                wr = add(wr, ws, -alpha)
                vr[h] = residual
                vs[h] = step
                vp[h] = direction
                trp[h] = mine
                tsp[h] = step_image
                vx[h] = alpha * direction if g == 1 else vx[h] + alpha * direction
            else:
                vx[h] += alpha * direction
                base[h] = base[h] - (tx[h] + alpha * (tr[h] + beta * tp[h]))
            gamma_was, alpha_was = gamma, alpha

    chains = (chain(0), chain(1))

    def go(which):
        next(chains[which], None)

    go(0)
    go(0)
    go(1)
    go(1)
    for copy in flex_copies:
        copy.wait()
    for copy in shared_copies:
        copy.wait_recv()
    lax.fori_loop(0, 2 * CHIPS, split_flex, 0)
    go(0)
    go(0)
    go(1)
    go(1)
    go(0)
    pick_columns(0)
    go(1)
    pick_columns(1)
    go(0)
    go(1)
    go(0)
    go(0)
    go(1)
    go(1)
    for _ in range(ITERS - 2):
        for which in (0, 1, 0, 1, 0, 0, 1, 1):
            go(which)
    for which in (0, 1, 0, 1, 0, 0, 0, 1, 1, 0, 1, 1, 0, 0, 1, 1):
        go(which)

    side = low_lanes(ROWS)
    trace_out[0] = jnp.where(side, base[0], base[1])
    for b in range(3):
        band = slice(b * SHARE, (b + 1) * SHARE)
        lower, upper = vx[0, band, :], vx[1, band, :]
        sign = sgn[band, :]
        lower, upper = sign * lower, sign * upper
        mult_out[0, b] = jnp.where(left_band, lower, swap(upper))
        mult_out[0, b + 3] = jnp.where(left_band, swap(lower), upper)

    for copy in pending:
        copy.wait_send()


def settle(mult, trace, mult_out, trace_out):
    mult_out[...] = mult[...]
    trace_out[...] = trace[...]


def body(edge_mid, edge_dir, seg_mid, seg_vec, currents, flexibility, partner, edge_block):
    vmem = pl.BlockSpec(memory_space=pltpu.VMEM)
    smem = pl.BlockSpec(memory_space=pltpu.SMEM)
    dma = pltpu.SemaphoreType.DMA
    half = CHIPS * ROWS

    def room(*shape):
        return pltpu.VMEM(shape, f32)

    def short(*shape):
        return pltpu.VMEM(shape, bf16)
    both = 2 * ITERS
    scratch = [
        room(CHIPS, 8, ROWS), room(2, 8, ROWS),
        room(2, CHIPS, LANES, LANES),
        room(2, CHIPS, LANES, LANES),
        room(both, CHIPS, MSG, LANES),
        room(2, CHIPS, 8, LANES),
        room(18, LANES + 8, LANES), room(18, LANES + 8, LANES),
        room(12, MSG, LANES), room(12, MSG, LANES), room(2, 8, LANES), room(2, 8, LANES),
    ]
    scratch += [room(6, MSG, LANES)] * both
    scratch += [room(2, 16, 8, LANES), room(both, 2, MSG, LANES), room(both, 2, MSG, LANES)]
    scratch += [
        room(2, ROWS, half), short(2, ROWS, half), short(2, ROWS, half),
        short(2, ROWS, DEPTH), short(2, ROWS, DEPTH),
        short(2, PICKS, DEPTH), short(2, PICKS, DEPTH), room(2, ROWS, LANES),
        short(2, ROWS, half), short(2, ROWS, half),
        short(2, half, LANES), short(2, DEPTH, LANES),
        room(ROWS, ROWS), room(ROWS, ROWS), short(PICKS, ROWS), room(ROWS, ROWS),
        room(LANES, ROWS), room(2, 6, ROWS, LANES),
        room(BAND, LANES), room(BAND, LANES),
    ]
    scratch += [room(2, ROWS, LANES)] * 4
    scratch += [room(2, BAND, LANES)] * 6
    scratch += [
        dma((8,)), dma((8,)), dma((8,)), dma, dma, dma((7,)), dma((7,)),
        dma((14, 7)), dma((14, 7)), dma((20,)), dma((20,)),
        dma((8, 5)), dma((8, 5)), dma((8, 2)), dma((8, 2)), dma((2, 15)), dma((2, 15)),
    ]
    outs = (
        jax.ShapeDtypeStruct((1, ROUNDS, SHARE, LANES), f32),
        jax.ShapeDtypeStruct((1, ROWS, LANES), f32),
    )
    solved = pl.pallas_call(
        kernel,
        out_shape=outs,
        in_specs=[vmem] * 5 + [smem] * 2 + [pl.BlockSpec(memory_space=pl.ANY)],
        out_specs=(vmem, vmem),
        scratch_shapes=scratch,
        compiler_params=pltpu.CompilerParams(
            collective_id=0, has_side_effects=True, vmem_limit_bytes=56 * 1024 * 1024),
        name="interface_cg",
    )(jnp.transpose(edge_mid, (1, 0, 2)), jnp.transpose(edge_dir, (1, 0, 2)),
      seg_mid, seg_vec, currents, partner, edge_block, flexibility)
    return pl.pallas_call(
        settle,
        out_shape=outs,
        in_specs=[vmem] * 2,
        out_specs=(vmem, vmem),
        name="settle",
    )(*solved)


def solution(mesh):
    in_specs = (
        P("sub", None, "seg"),
        P("sub", None, "seg"),
        P(None, "seg"),
        P(None, "seg"),
        P(None, "seg"),
        P("sub", "seg", None),
        P(),
        P(None, "sub", None),
    )
    out_specs = (P("sub", None, "seg", None), P("sub", "seg", None))
    return jax.shard_map(body, mesh=mesh, in_specs=in_specs, out_specs=out_specs, check_vma=False)
```

```python
import jax
import jax.numpy as jnp
from jax import lax
from jax.experimental import pallas as pl
from jax.experimental.pallas import tpu as pltpu
from jax.sharding import PartitionSpec as P

ITERS = 4
ROUNDS = 6
SHARE = 24
PICKS = ROUNDS * SHARE
BAND = PICKS // 2
MSG = BAND + 8
ROWS = 256
LANES = 128
HALF = LANES // 2
CHIPS = 8
MAIN = CHIPS * LANES
DEPTH = CHIPS * PICKS
CORE2 = 0.05 * 0.05
f32 = jnp.float32
bf16 = jnp.bfloat16
MESH = pl.DeviceIdType.MESH

PLANE = ((0, 1), (1, 0), (-1, 0), (1, 1), (-1, 1), (2, 0), (2, 1))
NEAR = ((0, 1), (1, 0), (-1, 0), (1, 1), (-1, 1))
FAR = (3, -3)
COLUMN = tuple((dz, fy) for dz in (4, -3, 3, -2, 2, -1, 1, 0) for fy in (1, 0) if dz or fy)


def split2(value):
    high = value.astype(bf16)
    return high, (value - high.astype(f32)).astype(bf16)


def dot(a, b):
    return jnp.dot(a, b, preferred_element_type=f32)


def kernel(em, ed, sm, sv, cur, part, eb, flex,
           mult_out, trace_out,
           geo, ge, cg, sg, xg, fg, ps, pr, pps, ppr, fps, fpr,
           wa0, wa1, wa2, wa3, wb0, wb1, wb2, wb3, fw, far_s, far_r,
           fv, fhi, flo, fsh, fsl, fssh, fssl, rem, kh, kl, cb, xb, pt, pk, ptb, pb, est, ebc,
           sgn, own, base, tx, tr, tp, trp, tsp, vr, vs, vp, vx,
           fsem, fsend, frecv, esend, erecv, gsend, grecv, dsend, drecv, psend, precv,
           nsend, nrecv, zsend, zrecv, asend, arecv):
    seg = lax.axis_index("seg")
    sub = lax.axis_index("sub")
    x, ylo, c = seg // 4, (seg // 2) % 2, seg % 2
    z, yh = sub // 2, sub % 2
    q = seg // 2
    windows = ((wa0, wa1, wa2, wa3), (wb0, wb1, wb2, wb3))

    def plane_dev(dx, fy, fc):
        yy = 1 - ylo if fy else ylo
        cc = 1 - c if fc else c
        return (((x + dx + 4) % 4) * 4 + yy * 2 + cc, sub)

    def column_dev(dz, fy):
        yy = 1 - yh if fy else yh
        return (seg, ((z + dz + 8) % 8) * 2 + yy)

    def chip_from(dx, fy):
        yy = 1 - ylo if fy else ylo
        return ((x - dx + 4) % 4) * 2 + yy

    def remote(src, dst, ss, rs, dev):
        return pltpu.make_async_remote_copy(
            src_ref=src, dst_ref=dst, send_sem=ss, recv_sem=rs, device_id=dev, device_id_type=MESH)

    pending = []
    sibling = plane_dev(0, 0, 1)

    def low_lanes(rows):
        return lax.broadcasted_iota(jnp.int32, (rows, LANES), 1) < HALF

    def swap(value):
        return pltpu.roll(value, HALF, 1)

    flex_copies = []
    for chip in range(CHIPS):
        src = flex.at[0, :, pl.ds(pl.multiple_of((chip * 2 + c) * ROWS, ROWS), ROWS)]
        copy = pltpu.make_async_copy(src, fv.at[c, :, chip * ROWS:(chip + 1) * ROWS], fsem.at[chip])
        copy.start()
        flex_copies.append(copy)
    barrier = pltpu.get_barrier_semaphore()
    peers = [plane_dev(dx, fy, 0) for dx, fy in PLANE] + [sibling]
    peers += [column_dev(dz, fy) for dz, fy in COLUMN]
    for peer in peers:
        pl.semaphore_signal(barrier, inc=1, device_id=peer, device_id_type=MESH)
    geo[q, 0:3, :] = sm[...]
    geo[q, 3:6, :] = sv[...]
    geo[q, 6:8, :] = jnp.zeros((2, ROWS), f32)
    for comp in range(3):
        ge[c, comp:comp + 1, :] = em[comp]
        ge[c, 3 + comp:4 + comp, :] = ed[comp]
    ge[c, 6:8, :] = jnp.zeros((2, ROWS), f32)
    turned = cur[...].T
    left = low_lanes(LANES)
    cg[0, q] = jnp.where(left, turned[:LANES], swap(turned[LANES:]))
    cg[1, q] = jnp.where(left, swap(turned[:LANES]), turned[LANES:])
    pl.semaphore_wait(barrier, len(peers))

    edge_copy = remote(ge.at[c], ge.at[c], esend, erecv, sibling)
    edge_copy.start()
    pending.append(edge_copy)
    geo_copies = []
    for k, (dx, fy) in enumerate(PLANE):
        copy = remote(geo.at[q], geo.at[q], gsend.at[k], grecv.at[k], plane_dev(dx, fy, 0))
        copy.start()
        geo_copies.append(copy)
    pending.extend(geo_copies)

    def gather_start(buf, g):
        mine = buf.at[q]
        for k, (dx, fy) in enumerate(PLANE):
            copy = remote(mine, mine, dsend.at[g, k], drecv.at[g, k], plane_dev(dx, fy, 0))
            copy.start()
            pending.append(copy)

    def gather_wait(buf, g, each):
        each(q)
        for k, (dx, fy) in enumerate(PLANE):
            origin = chip_from(dx, fy)
            here = buf.at[origin]
            remote(here, here, dsend.at[g, k], drecv.at[g, k], sibling).wait_recv()
            each(origin)

    gather_start(cg.at[0], 0)
    gather_start(cg.at[1], 1)
    shared_copies = []
    for chip in range(CHIPS):
        src = flex.at[0, :, pl.ds(pl.multiple_of((chip * 2 + 1 - c) * ROWS, ROWS), ROWS)]
        dst = fv.at[c, :, chip * ROWS:(chip + 1) * ROWS]
        copy = remote(src, dst, fsend.at[chip], frecv.at[chip], sibling)
        copy.start()
        shared_copies.append(copy)
    pending.extend(shared_copies)

    lane_at = lax.broadcasted_iota(jnp.int32, (1, ROWS), 1)
    pt[...] = jnp.zeros((ROWS, ROWS), f32)
    pk[...] = jnp.zeros((ROWS, ROWS), f32)

    def hot_row(k, carry):
        row = jnp.where(lane_at == eb[k // SHARE, 0, k % SHARE], 1.0, 0.0).astype(f32)
        upper = k // BAND
        at = k - upper * BAND
        place = jnp.where(at < HALF, upper * HALF + at, LANES + upper * 8 + at - HALF)
        pt[pl.ds(k, 1), :] = row
        pk[pl.ds(place, 1), :] = row
        return carry
    lax.fori_loop(0, PICKS, hot_row, 0)
    ptb[...] = pt[0:PICKS, :].astype(bf16)
    pb[...] = pk[...].T

    edge_copy.wait_recv()
    for side in range(2):
        est[...] = jnp.zeros((LANES, ROWS), f32)
        est[0:8, :] = ge[side]
        columns = est[...].T
        for comp in range(6):
            ebc[side, comp] = jnp.broadcast_to(columns[:, comp:comp + 1], (ROWS, LANES))

    left_band = low_lanes(SHARE)
    for b in range(3):
        band = slice(b * SHARE, (b + 1) * SHARE)
        first = jnp.where(part[b, sub] > sub, 1.0, 0.0).astype(f32)
        second = jnp.where(part[b + 3, sub] > sub, 1.0, 0.0).astype(f32)
        mark = jnp.where(left_band, first, second)
        own[band, :] = mark
        sgn[band, :] = mark * 2.0 - 1.0

    for copy in geo_copies:
        copy.wait_recv()

    def tile(step, carry):
        side, chip = step // CHIPS, step % CHIPS
        for h in range(2):
            row = [geo[chip, pl.ds(comp, 1), h * LANES:(h + 1) * LANES] for comp in range(6)]
            lanes = pl.ds(pl.multiple_of(chip * ROWS + h * LANES, LANES), LANES)
            for part_at in range(4):
                rows = slice(part_at * 64, part_at * 64 + 64)
                dist = jnp.full((64, LANES), CORE2, f32)
                along = jnp.zeros((64, LANES), f32)
                for comp in range(3):
                    gap = ebc[side, comp, rows, :] - row[comp]
                    dist = dist + gap * gap
                    along = along + ebc[side, 3 + comp, rows, :] * row[3 + comp]
                high, low = split2(along * lax.rsqrt(dist))
                kh[side, rows, lanes] = high
                kl[side, rows, lanes] = low
        return carry
    lax.fori_loop(0, 2 * CHIPS, tile, 0)

    def unpack(value):
        high = value.astype(bf16).astype(f32)
        low = value - high
        side = low_lanes(value.shape[0])
        return jnp.where(side, high, swap(low)), jnp.where(side, swap(high), low)

    def dense_block(buf, h):
        def each(chip):
            one, two = unpack(buf[chip])
            cb[h, pl.ds(pl.multiple_of(chip * ROWS, LANES), LANES), :] = one.astype(bf16)
            cb[h, pl.ds(pl.multiple_of(chip * ROWS + LANES, LANES), LANES), :] = two.astype(bf16)
        return each

    def dense_dot(high, low, h):
        def rows_of(side):
            return dot(high[side], cb[h]) + dot(low[side], cb[h])
        return rows_of

    def combine(inst, rows_of, scalars):
        other = rows_of(1 - c)
        other = other + swap(other)
        ps[inst, 0:LANES, :] = jnp.where(left, other[:LANES], other[LANES:])
        ps[inst, LANES:LANES + 8, :] = scalars
        copy = remote(ps.at[inst], pr.at[inst], psend.at[inst], precv.at[inst], sibling)
        copy.start()
        pending.append(copy)
        mine = rows_of(c)
        mine = mine + swap(mine)
        copy.wait_recv()
        got = pr[inst, 0:LANES, :]
        back = swap(got)
        top = mine[:LANES] + jnp.where(left, got, back)
        bottom = mine[LANES:] + jnp.where(left, back, got)
        return jnp.concatenate([top, bottom], axis=0), scalars + pr[inst, LANES:LANES + 8, :]

    def split_flex(step, carry):
        side, chip = step // CHIPS, step % CHIPS
        for h in range(2):
            lanes = pl.ds(pl.multiple_of(chip * ROWS + h * LANES, LANES), LANES)
            high, low = split2(fv[side, :, lanes])
            fhi[side, :, lanes] = high
            flo[side, :, lanes] = low
        return carry

    def pick_columns(half):
        rem[...] = jnp.zeros((2, ROWS, LANES), f32)

        def one(chip, carry):
            tail = pltpu.roll(pb[:, LANES:], chip * (PICKS - LANES), 1)
            choose = jnp.concatenate([pb[:, :LANES], tail], axis=1).astype(bf16)
            src = pl.ds(pl.multiple_of(chip * ROWS, ROWS), ROWS)
            dst = pl.ds(pl.multiple_of(chip * LANES, LANES), LANES)
            for at, (whole, out) in enumerate(((fhi, fsh), (flo, fsl))):
                got = dot(whole[half, :, src], choose)
                out[half, :, dst] = got[:, :LANES].astype(bf16)
                rem[at] += got[:, LANES:]
            return carry
        lax.fori_loop(0, CHIPS, one, 0)
        fsh[half, :, MAIN:] = rem[0].astype(bf16)
        fsl[half, :, MAIN:] = rem[1].astype(bf16)
        fssh[half] = dot(ptb[...], fsh[half]).astype(bf16)
        fssl[half] = dot(ptb[...], fsl[half]).astype(bf16)

    def pick_rows(full):
        high = full.astype(bf16)
        rest = full - high.astype(f32)
        mid = rest.astype(bf16)
        low = (rest - mid.astype(f32)).astype(bf16)
        both = dot(ptb[...], jnp.where(low_lanes(ROWS), high.astype(f32), mid.astype(f32)).astype(bf16))
        picked = (both + swap(both)) + dot(ptb[...], low)
        return jnp.where(low_lanes(BAND), picked[:BAND], picked[BAND:])

    def near_slot(dz, fy):
        return (dz + 1) * 2 + fy

    def near_start(buf, e):
        mine = buf.at[near_slot(0, 0)]
        for k, (dz, fy) in enumerate(NEAR):
            copy = remote(mine, buf.at[near_slot(-dz, fy)], nsend.at[e, k], nrecv.at[e, k], column_dev(dz, fy))
            copy.start()
            pending.append(copy)

    def near_wait(buf, e):
        for k, (dz, fy) in enumerate(NEAR):
            here = buf.at[near_slot(-dz, fy)]
            remote(here, here, nsend.at[e, k], nrecv.at[e, k], column_dev(dz, fy)).wait_recv()

    def far_start(src, dst, e):
        for t, dz in enumerate(FAR):
            copy = remote(src.at[t], dst.at[t], zsend.at[e, t], zrecv.at[e, t], column_dev(dz, 0))
            copy.start()
            pending.append(copy)

    def far_wait(dst, e):
        for t, dz in enumerate(FAR):
            here = dst.at[t]
            remote(here, here, zsend.at[e, t], zrecv.at[e, t], column_dev(dz, 0)).wait_recv()

    def place_of(r, at):
        p = part[r, at]
        rel = (p // 2 - z + 8) % 8
        shifted = (rel + 1) % 8
        slot = shifted * 2 + jnp.where(p % 2 == yh, 0, 1)
        inside = shifted < 3
        return rel, inside, jnp.where(inside, slot, 0)

    far_places = [[place_of(r, ((z + dz + 8) % 8) * 2 + yh)[2] for r in range(ROUNDS)] for dz in FAR]
    my_places = [place_of(r, sub) for r in range(ROUNDS)]

    def sums_far(buf, dst, at):
        keep = [buf[s, at:at + 8, :] for s in range(6)]
        upper = (keep[2] + keep[3]) + (keep[4] + keep[5])
        whole = upper + (keep[0] + keep[1])
        dst[0, at:at + 8, :] = upper
        dst[1, at:at + 8, :] = whole
        return whole

    def sparse_write(packed, chip, h):
        one, two = unpack(packed)
        for at, value in ((0, one), (HALF, two)):
            rows = pl.ds(pl.multiple_of(chip * LANES + at, HALF), HALF)
            xb[h, rows, :] = value[:HALF].astype(bf16)
        tail = pl.ds(pl.multiple_of(MAIN + chip * 16, 16), 16)
        xb[h, tail, :] = jnp.concatenate([one[HALF:], two[HALF:]], axis=0).astype(bf16)

    def sparse_block(buf, h):
        def each(chip):
            sparse_write(buf[chip, 0:BAND, :], chip, h)
        return each

    def sparse_dot(h):
        def rows_of(side):
            return dot(fsh[side], xb[h]) + dot(fsl[side], xb[h])
        return rows_of

    def combine_picks(inst, h, scalars):
        left_pack = low_lanes(BAND)

        def rows_of(side):
            got = dot(fssh[side], xb[h]) + dot(fssl[side], xb[h])
            got = got + swap(got)
            return jnp.where(left_pack, got[:BAND], got[BAND:])
        pps[inst, 0:BAND, :] = rows_of(1 - c)
        pps[inst, BAND:MSG, :] = scalars
        copy = remote(pps.at[inst], ppr.at[inst], psend.at[inst], precv.at[inst], sibling)
        copy.start()
        pending.append(copy)
        mine = rows_of(c)
        copy.wait_recv()
        return mine + ppr[inst, 0:BAND, :], scalars + ppr[inst, BAND:MSG, :]

    def add(first, second, scale):
        out = dict(first)
        for key, value in second.items():
            out[key] = out[key] + scale * value if key in out else scale * value
        return out

    def full_rows(inst, h, weights):
        for chip in range(CHIPS):
            value = None
            for g, weight in weights.items():
                term = weight * xg[g * 2 + h, chip, 0:BAND, :]
                value = term if value is None else value + term
            sparse_write(value, chip, h)
        return combine(inst, sparse_dot(h), zeros8)[0]

    zeros8 = jnp.zeros((8, LANES), f32)

    def inner_rows(residual, image):
        gamma = jnp.sum(own[...] * residual * residual, axis=0, keepdims=True)
        delta = jnp.sum(residual * image, axis=0, keepdims=True)
        return jnp.concatenate([gamma, delta, jnp.zeros((6, LANES), f32)], axis=0)

    def chain(h):
        gather_wait(cg.at[h], h, dense_block(cg.at[h], h))
        yield
        total, _ = combine(h, dense_dot(kh, kl, h), zeros8)
        sg[h, q] = jnp.where(left, total[:LANES], total[LANES:])
        gather_start(sg.at[h], 2 + h)
        yield
        gather_wait(sg.at[h], 2 + h, dense_block(sg.at[h], h))
        yield
        total, _ = combine(2 + h, dense_dot(fhi, flo, h), zeros8)
        base[h] = total
        mine = pick_rows(total)
        scalars = zeros8
        gamma_was = alpha_was = None
        for g in range(ITERS + 1):
            e = g * 2 + h
            if g == ITERS:
                fw[h, len(COLUMN)] = scalars
                for k, (dz, fy) in enumerate(COLUMN):
                    copy = remote(fw.at[h, len(COLUMN)], fw.at[h, k], asend.at[h, k], arecv.at[h, k], column_dev(dz, fy))
                    copy.start()
                    pending.append(copy)
                yield
                tx[h] = full_rows(12 + 3 * h, h, wx)
                tr[h] = full_rows(13 + 3 * h, h, wr)
                tp[h] = full_rows(14 + 3 * h, h, wp)
                yield
                sums = scalars
                for k, (dz, fy) in enumerate(COLUMN):
                    here = fw.at[h, k]
                    remote(here, here, asend.at[h, k], arecv.at[h, k], column_dev(dz, fy)).wait_recv()
                    sums = sums + fw[h, k]
                fg[h, q] = sums
                gather_start(fg.at[h], 12 + h)
                yield
                gather_wait(fg.at[h], 12 + h, lambda chip: None)
                sums = zeros8
                for chip in range(CHIPS):
                    sums = sums + fg[h, chip]
                fps[h] = sums
                copy = remote(fps.at[h], fpr.at[h], psend.at[18 + h], precv.at[18 + h], sibling)
                copy.start()
                pending.append(copy)
                yield
                copy.wait_recv()
                sums = sums + fpr[h]
            else:
                buf = windows[h][g]
                buf[near_slot(0, 0), 0:BAND, :] = mine
                buf[near_slot(0, 0), BAND:MSG, :] = scalars
                near_start(buf, e)
                yield
                near_wait(buf, e)
                for t in range(2):
                    for b in range(3):
                        band = slice(b * SHARE, (b + 1) * SHARE)
                        far_s[e, t, band, :] = jnp.where(
                            left_band, buf[far_places[t][b], band, :], buf[far_places[t][b + 3], band, :])
                whole = sums_far(buf, far_s.at[e], BAND)
                far_start(far_s.at[e], far_r.at[e], e)
                yield
                far_wait(far_r.at[e], e)
                pieces = []
                for b in range(3):
                    band = slice(b * SHARE, (b + 1) * SHARE)
                    sides = []
                    for r in (b, b + 3):
                        rel, inside, slot = my_places[r]
                        away = jnp.where(rel < 5, far_r[e, 1, band, :], far_r[e, 0, band, :])
                        sides.append(jnp.where(inside, buf[slot, band, :], away))
                    pieces.append(mine[band, :] - jnp.where(left_band, sides[0], sides[1]))
                vector = jnp.concatenate(pieces, axis=0)
                xg[e, q, 0:BAND, :] = vector
                xg[e, q, BAND:MSG, :] = whole + far_r[e, 0, BAND:MSG, :] + far_r[e, 1, BAND:MSG, :]
                gather_start(xg.at[e], 4 + e)
                yield
                gather_wait(xg.at[e], 4 + e, sparse_block(xg.at[e], h))
                yield
                sums = zeros8
                for chip in range(CHIPS):
                    sums = sums + xg[e, chip, BAND:MSG, :]
                applied, sums = combine_picks(4 + e, h, sums)
            if g == 0:
                vr[h] = vector
                trp[h] = applied
                mine = applied
                scalars = inner_rows(vector, mine)
                wr = {0: jnp.ones((1, LANES), f32)}
                continue
            sums = sums + swap(sums)
            gamma, delta = sums[0:1], sums[1:2]
            residual = vr[h]
            if g == 1:
                alpha = gamma / delta
                step, direction, step_image = vector, residual, applied
                wp, ws = wr, {}
            else:
                beta = gamma / gamma_was
                alpha = gamma / (delta - beta * gamma / alpha_was)
                direction = residual + beta * vp[h]
                if g < ITERS:
                    step = vector + beta * vs[h]
                    step_image = applied + beta * tsp[h]
                    wp = add(wr, wp, beta)
                    ws = add({}, ws, beta)
            if g < ITERS:
                mine = trp[h] - alpha * step_image
                residual = residual - alpha * step
                scalars = inner_rows(residual, mine)
                ws[g] = jnp.ones((1, LANES), f32)
                wx = add(wx if g > 1 else {}, wp, alpha)
                wr = add(wr, ws, -alpha)
                vr[h] = residual
                vs[h] = step
                vp[h] = direction
                trp[h] = mine
                tsp[h] = step_image
                vx[h] = alpha * direction if g == 1 else vx[h] + alpha * direction
            else:
                vx[h] += alpha * direction
                base[h] = base[h] - (tx[h] + alpha * (tr[h] + beta * tp[h]))
            gamma_was, alpha_was = gamma, alpha

    chains = (chain(0), chain(1))

    def go(which):
        next(chains[which], None)

    for copy in flex_copies:
        copy.wait()
    for copy in shared_copies:
        copy.wait_recv()
    lax.fori_loop(0, 2 * CHIPS, split_flex, 0)
    go(0)
    go(0)
    pick_columns(0)
    go(1)
    go(1)
    pick_columns(1)
    for which in (0, 0, 1, 1, 0, 1, 0, 1, 0, 0, 1, 1):
        go(which)
    for _ in range(ITERS - 2):
        for which in (0, 1, 0, 1, 0, 0, 1, 1):
            go(which)
    for which in (0, 1, 0, 1, 0, 0, 0, 1, 1, 0, 1, 1, 0, 0, 1, 1):
        go(which)

    side = low_lanes(ROWS)
    trace_out[0] = jnp.where(side, base[0], base[1])
    for b in range(3):
        band = slice(b * SHARE, (b + 1) * SHARE)
        lower, upper = vx[0, band, :], vx[1, band, :]
        sign = sgn[band, :]
        lower, upper = sign * lower, sign * upper
        mult_out[0, b] = jnp.where(left_band, lower, swap(upper))
        mult_out[0, b + 3] = jnp.where(left_band, swap(lower), upper)

    for copy in pending:
        copy.wait_send()


def settle(mult, trace, mult_out, trace_out):
    mult_out[...] = mult[...]
    trace_out[...] = trace[...]


def body(edge_mid, edge_dir, seg_mid, seg_vec, currents, flexibility, partner, edge_block):
    vmem = pl.BlockSpec(memory_space=pltpu.VMEM)
    smem = pl.BlockSpec(memory_space=pltpu.SMEM)
    dma = pltpu.SemaphoreType.DMA
    half = CHIPS * ROWS

    def room(*shape):
        return pltpu.VMEM(shape, f32)

    def short(*shape):
        return pltpu.VMEM(shape, bf16)
    both = 2 * ITERS
    scratch = [
        room(CHIPS, 8, ROWS), room(2, 8, ROWS),
        room(2, CHIPS, LANES, LANES),
        room(2, CHIPS, LANES, LANES),
        room(both, CHIPS, MSG, LANES),
        room(2, CHIPS, 8, LANES),
        room(18, LANES + 8, LANES), room(18, LANES + 8, LANES),
        room(12, MSG, LANES), room(12, MSG, LANES), room(2, 8, LANES), room(2, 8, LANES),
    ]
    scratch += [room(6, MSG, LANES)] * both
    scratch += [room(2, 16, 8, LANES), room(both, 2, MSG, LANES), room(both, 2, MSG, LANES)]
    scratch += [
        room(2, ROWS, half), short(2, ROWS, half), short(2, ROWS, half),
        short(2, ROWS, DEPTH), short(2, ROWS, DEPTH),
        short(2, PICKS, DEPTH), short(2, PICKS, DEPTH), room(2, ROWS, LANES),
        short(2, ROWS, half), short(2, ROWS, half),
        short(2, half, LANES), short(2, DEPTH, LANES),
        room(ROWS, ROWS), room(ROWS, ROWS), short(PICKS, ROWS), room(ROWS, ROWS),
        room(LANES, ROWS), room(2, 6, ROWS, LANES),
        room(BAND, LANES), room(BAND, LANES),
    ]
    scratch += [room(2, ROWS, LANES)] * 4
    scratch += [room(2, BAND, LANES)] * 6
    scratch += [
        dma((8,)), dma((8,)), dma((8,)), dma, dma, dma((7,)), dma((7,)),
        dma((14, 7)), dma((14, 7)), dma((20,)), dma((20,)),
        dma((8, 5)), dma((8, 5)), dma((8, 2)), dma((8, 2)), dma((2, 15)), dma((2, 15)),
    ]
    outs = (
        jax.ShapeDtypeStruct((1, ROUNDS, SHARE, LANES), f32),
        jax.ShapeDtypeStruct((1, ROWS, LANES), f32),
    )
    solved = pl.pallas_call(
        kernel,
        out_shape=outs,
        in_specs=[vmem] * 5 + [smem] * 2 + [pl.BlockSpec(memory_space=pl.ANY)],
        out_specs=(vmem, vmem),
        scratch_shapes=scratch,
        compiler_params=pltpu.CompilerParams(
            collective_id=0, has_side_effects=True, vmem_limit_bytes=56 * 1024 * 1024),
        name="interface_cg",
    )(jnp.transpose(edge_mid, (1, 0, 2)), jnp.transpose(edge_dir, (1, 0, 2)),
      seg_mid, seg_vec, currents, partner, edge_block, flexibility)
    return pl.pallas_call(
        settle,
        out_shape=outs,
        in_specs=[vmem] * 2,
        out_specs=(vmem, vmem),
        name="settle",
    )(*solved)


def solution(mesh):
    in_specs = (
        P("sub", None, "seg"),
        P("sub", None, "seg"),
        P(None, "seg"),
        P(None, "seg"),
        P(None, "seg"),
        P("sub", "seg", None),
        P(),
        P(None, "sub", None),
    )
    out_specs = (P("sub", None, "seg", None), P("sub", "seg", None))
    return jax.shard_map(body, mesh=mesh, in_specs=in_specs, out_specs=out_specs, check_vma=False)
```

```python
import jax
import jax.numpy as jnp
from jax import lax
from jax.experimental import pallas as pl
from jax.experimental.pallas import tpu as pltpu
from jax.sharding import PartitionSpec as P

ITERS = 4
ROUNDS = 6
SHARE = 24
PICKS = ROUNDS * SHARE
BAND = PICKS // 2
MSG = BAND + 8
ROWS = 256
LANES = 128
HALF = LANES // 2
CHIPS = 8
MAIN = CHIPS * LANES
DEPTH = CHIPS * PICKS
CORE2 = 0.05 * 0.05
f32 = jnp.float32
bf16 = jnp.bfloat16
MESH = pl.DeviceIdType.MESH

PLANE = ((0, 1), (1, 0), (-1, 0), (1, 1), (-1, 1), (2, 0), (2, 1))
ALONG = (1, -1, 2)
NEAR = ((0, 1), (1, 0), (-1, 0), (1, 1), (-1, 1))
FAR = (3, -3)
COLUMN = tuple((dz, fy) for dz in (4, -3, 3, -2, 2, -1, 1, 0) for fy in (1, 0) if dz or fy)


def split2(value):
    high = value.astype(bf16)
    return high, (value - high.astype(f32)).astype(bf16)


def dot(a, b):
    return jnp.dot(a, b, preferred_element_type=f32)


def kernel(em, ed, sm, sv, cur, part, eb, flex,
           mult_out, trace_out,
           geo, ge, cg, sg, xg, fg, ps, pr, pps, ppr, fps, fpr, cps, cpr, yps, ypr,
           wa0, wa1, wa2, wa3, wb0, wb1, wb2, wb3, fw, far_s, far_r,
           fv, fhi, flo, fsh, fsl, fssh, fssl, rem, kh, kl, cb, xb, pt, pk, ptb, pb, est, ebc,
           sgn, own, base, tx, tr, tp, trp, tsp, vr, vs, vp, vx,
           fsem, fsend, frecv, esend, erecv, gsend, grecv, dsend, drecv, psend, precv, ysend, yrecv,
           nsend, nrecv, zsend, zrecv, asend, arecv):
    seg = lax.axis_index("seg")
    sub = lax.axis_index("sub")
    x, ylo, c = seg // 4, (seg // 2) % 2, seg % 2
    z, yh = sub // 2, sub % 2
    q = seg // 2
    windows = ((wa0, wa1, wa2, wa3), (wb0, wb1, wb2, wb3))

    def plane_dev(dx, fy, fc):
        yy = 1 - ylo if fy else ylo
        cc = 1 - c if fc else c
        return (((x + dx + 4) % 4) * 4 + yy * 2 + cc, sub)

    def column_dev(dz, fy):
        yy = 1 - yh if fy else yh
        return (seg, ((z + dz + 8) % 8) * 2 + yy)

    def chip_from(dx, fy):
        yy = 1 - ylo if fy else ylo
        return ((x - dx + 4) % 4) * 2 + yy

    def remote(src, dst, ss, rs, dev):
        return pltpu.make_async_remote_copy(
            src_ref=src, dst_ref=dst, send_sem=ss, recv_sem=rs, device_id=dev, device_id_type=MESH)

    pending = []
    sibling = plane_dev(0, 0, 1)

    def low_lanes(rows):
        return lax.broadcasted_iota(jnp.int32, (rows, LANES), 1) < HALF

    def swap(value):
        return pltpu.roll(value, HALF, 1)

    flex_copies = []
    for chip in range(CHIPS):
        src = flex.at[0, :, pl.ds(pl.multiple_of((chip * 2 + c) * ROWS, ROWS), ROWS)]
        copy = pltpu.make_async_copy(src, fv.at[c, :, chip * ROWS:(chip + 1) * ROWS], fsem.at[chip])
        copy.start()
        flex_copies.append(copy)
    barrier = pltpu.get_barrier_semaphore()
    peers = [plane_dev(dx, fy, 0) for dx, fy in PLANE] + [sibling, plane_dev(0, 1, 1)]
    peers += [column_dev(dz, fy) for dz, fy in COLUMN]
    for peer in peers:
        pl.semaphore_signal(barrier, inc=1, device_id=peer, device_id_type=MESH)
    geo[x, 0:3, :] = sm[...]
    geo[x, 3:6, :] = sv[...]
    geo[x, 6:8, :] = jnp.zeros((2, ROWS), f32)
    my_set = ylo * 2 + c
    for comp in range(3):
        ge[my_set, comp:comp + 1, :] = em[comp]
        ge[my_set, 3 + comp:4 + comp, :] = ed[comp]
    ge[my_set, 6:8, :] = jnp.zeros((2, ROWS), f32)
    turned = cur[...].T
    left = low_lanes(LANES)
    cg[0, x] = jnp.where(left, turned[:LANES], swap(turned[LANES:]))
    cg[1, x] = jnp.where(left, swap(turned[:LANES]), turned[LANES:])
    pl.semaphore_wait(barrier, len(peers))

    edge_copies = []
    for k, (fy, fc) in enumerate(((0, 1), (1, 0), (1, 1))):
        copy = remote(ge.at[my_set], ge.at[my_set], esend.at[k], erecv.at[k], plane_dev(0, fy, fc))
        copy.start()
        edge_copies.append(copy)
    geo_copies = []
    for k, dx in enumerate(ALONG):
        copy = remote(geo.at[x], geo.at[x], gsend.at[k], grecv.at[k], plane_dev(dx, 0, 0))
        copy.start()
        geo_copies.append(copy)
    pending.extend(edge_copies + geo_copies)

    def along_start(h):
        for k, dx in enumerate(ALONG):
            copy = remote(cg.at[h, x], cg.at[h, x], dsend.at[h, k], drecv.at[h, k], plane_dev(dx, 0, 0))
            copy.start()
            pending.append(copy)

    def along_wait(h, each):
        each(x)
        for k, dx in enumerate(ALONG):
            origin = (x - dx + 4) % 4
            here = cg.at[h, origin]
            remote(here, here, dsend.at[h, k], drecv.at[h, k], sibling).wait_recv()
            each(origin)

    def gather_start(buf, g):
        mine = buf.at[q]
        for k, (dx, fy) in enumerate(PLANE):
            copy = remote(mine, mine, dsend.at[g, k], drecv.at[g, k], plane_dev(dx, fy, 0))
            copy.start()
            pending.append(copy)

    def gather_wait(buf, g, each):
        each(q)
        for k, (dx, fy) in enumerate(PLANE):
            origin = chip_from(dx, fy)
            here = buf.at[origin]
            remote(here, here, dsend.at[g, k], drecv.at[g, k], sibling).wait_recv()
            each(origin)

    along_start(0)
    along_start(1)
    shared_copies = []
    for chip in range(CHIPS):
        src = flex.at[0, :, pl.ds(pl.multiple_of((chip * 2 + 1 - c) * ROWS, ROWS), ROWS)]
        dst = fv.at[c, :, chip * ROWS:(chip + 1) * ROWS]
        copy = remote(src, dst, fsend.at[chip], frecv.at[chip], sibling)
        copy.start()
        shared_copies.append(copy)
    pending.extend(shared_copies)

    lane_at = lax.broadcasted_iota(jnp.int32, (1, ROWS), 1)
    pt[...] = jnp.zeros((ROWS, ROWS), f32)
    pk[...] = jnp.zeros((ROWS, ROWS), f32)

    def hot_row(k, carry):
        row = jnp.where(lane_at == eb[k // SHARE, 0, k % SHARE], 1.0, 0.0).astype(f32)
        upper = k // BAND
        at = k - upper * BAND
        place = jnp.where(at < HALF, upper * HALF + at, LANES + upper * 8 + at - HALF)
        pt[pl.ds(k, 1), :] = row
        pk[pl.ds(place, 1), :] = row
        return carry
    lax.fori_loop(0, PICKS, hot_row, 0)
    ptb[...] = pt[0:PICKS, :].astype(bf16)
    pb[...] = pk[...].T

    for copy in edge_copies:
        copy.wait_recv()
    for side in range(4):
        est[...] = jnp.zeros((LANES, ROWS), f32)
        est[0:8, :] = ge[side]
        columns = est[...].T
        for comp in range(6):
            ebc[side, comp] = jnp.broadcast_to(columns[:, comp:comp + 1], (ROWS, LANES))

    left_band = low_lanes(SHARE)
    for b in range(3):
        band = slice(b * SHARE, (b + 1) * SHARE)
        first = jnp.where(part[b, sub] > sub, 1.0, 0.0).astype(f32)
        second = jnp.where(part[b + 3, sub] > sub, 1.0, 0.0).astype(f32)
        mark = jnp.where(left_band, first, second)
        own[band, :] = mark
        sgn[band, :] = mark * 2.0 - 1.0

    for copy in geo_copies:
        copy.wait_recv()

    def tile(step, carry):
        side, chip = step // 4, step % 4
        for h in range(2):
            row = [geo[chip, pl.ds(comp, 1), h * LANES:(h + 1) * LANES] for comp in range(6)]
            lanes = pl.ds(pl.multiple_of(chip * ROWS + h * LANES, LANES), LANES)
            for part_at in range(4):
                rows = slice(part_at * 64, part_at * 64 + 64)
                dist = jnp.full((64, LANES), CORE2, f32)
                along = jnp.zeros((64, LANES), f32)
                for comp in range(3):
                    gap = ebc[side, comp, rows, :] - row[comp]
                    dist = dist + gap * gap
                    along = along + ebc[side, 3 + comp, rows, :] * row[3 + comp]
                high, low = split2(along * lax.rsqrt(dist))
                kh[side, rows, lanes] = high
                kl[side, rows, lanes] = low
        return carry
    lax.fori_loop(0, 16, tile, 0)

    def unpack(value):
        high = value.astype(bf16).astype(f32)
        low = value - high
        side = low_lanes(value.shape[0])
        return jnp.where(side, high, swap(low)), jnp.where(side, swap(high), low)

    def dense_block(buf, h):
        def each(chip):
            one, two = unpack(buf[chip])
            cb[h, pl.ds(pl.multiple_of(chip * ROWS, LANES), LANES), :] = one.astype(bf16)
            cb[h, pl.ds(pl.multiple_of(chip * ROWS + LANES, LANES), LANES), :] = two.astype(bf16)
        return each

    def dense_dot(high, low, h):
        def rows_of(side):
            return dot(high[side], cb[h]) + dot(low[side], cb[h])
        return rows_of

    def combine(inst, rows_of, scalars):
        other = rows_of(1 - c)
        other = other + swap(other)
        ps[inst, 0:LANES, :] = jnp.where(left, other[:LANES], other[LANES:])
        ps[inst, LANES:LANES + 8, :] = scalars
        copy = remote(ps.at[inst], pr.at[inst], psend.at[inst], precv.at[inst], sibling)
        copy.start()
        pending.append(copy)
        mine = rows_of(c)
        mine = mine + swap(mine)
        copy.wait_recv()
        got = pr[inst, 0:LANES, :]
        back = swap(got)
        top = mine[:LANES] + jnp.where(left, got, back)
        bottom = mine[LANES:] + jnp.where(left, back, got)
        return jnp.concatenate([top, bottom], axis=0), scalars + pr[inst, LANES:LANES + 8, :]

    def split_flex(step, carry):
        side, chip = step // CHIPS, step % CHIPS
        for h in range(2):
            lanes = pl.ds(pl.multiple_of(chip * ROWS + h * LANES, LANES), LANES)
            high, low = split2(fv[side, :, lanes])
            fhi[side, :, lanes] = high
            flo[side, :, lanes] = low
        return carry

    def pick_columns(half):
        rem[...] = jnp.zeros((2, ROWS, LANES), f32)

        def one(chip, carry):
            tail = pltpu.roll(pb[:, LANES:], chip * (PICKS - LANES), 1)
            choose = jnp.concatenate([pb[:, :LANES], tail], axis=1).astype(bf16)
            src = pl.ds(pl.multiple_of(chip * ROWS, ROWS), ROWS)
            dst = pl.ds(pl.multiple_of(chip * LANES, LANES), LANES)
            for at, (whole, out) in enumerate(((fhi, fsh), (flo, fsl))):
                got = dot(whole[half, :, src], choose)
                out[half, :, dst] = got[:, :LANES].astype(bf16)
                rem[at] += got[:, LANES:]
            return carry
        lax.fori_loop(0, CHIPS, one, 0)
        fsh[half, :, MAIN:] = rem[0].astype(bf16)
        fsl[half, :, MAIN:] = rem[1].astype(bf16)
        fssh[half] = dot(ptb[...], fsh[half]).astype(bf16)
        fssl[half] = dot(ptb[...], fsl[half]).astype(bf16)

    def pick_rows(full):
        high = full.astype(bf16)
        rest = full - high.astype(f32)
        mid = rest.astype(bf16)
        low = (rest - mid.astype(f32)).astype(bf16)
        both = dot(ptb[...], jnp.where(low_lanes(ROWS), high.astype(f32), mid.astype(f32)).astype(bf16))
        picked = (both + swap(both)) + dot(ptb[...], low)
        return jnp.where(low_lanes(BAND), picked[:BAND], picked[BAND:])

    def near_slot(dz, fy):
        return (dz + 1) * 2 + fy

    def near_start(buf, e):
        mine = buf.at[near_slot(0, 0)]
        for k, (dz, fy) in enumerate(NEAR):
            copy = remote(mine, buf.at[near_slot(-dz, fy)], nsend.at[e, k], nrecv.at[e, k], column_dev(dz, fy))
            copy.start()
            pending.append(copy)

    def near_wait(buf, e):
        for k, (dz, fy) in enumerate(NEAR):
            here = buf.at[near_slot(-dz, fy)]
            remote(here, here, nsend.at[e, k], nrecv.at[e, k], column_dev(dz, fy)).wait_recv()

    def far_start(src, dst, e):
        for t, dz in enumerate(FAR):
            copy = remote(src.at[t], dst.at[t], zsend.at[e, t], zrecv.at[e, t], column_dev(dz, 0))
            copy.start()
            pending.append(copy)

    def far_wait(dst, e):
        for t, dz in enumerate(FAR):
            here = dst.at[t]
            remote(here, here, zsend.at[e, t], zrecv.at[e, t], column_dev(dz, 0)).wait_recv()

    def place_of(r, at):
        p = part[r, at]
        rel = (p // 2 - z + 8) % 8
        shifted = (rel + 1) % 8
        slot = shifted * 2 + jnp.where(p % 2 == yh, 0, 1)
        inside = shifted < 3
        return rel, inside, jnp.where(inside, slot, 0)

    far_places = [[place_of(r, ((z + dz + 8) % 8) * 2 + yh)[2] for r in range(ROUNDS)] for dz in FAR]
    my_places = [place_of(r, sub) for r in range(ROUNDS)]

    def sums_far(buf, dst, at):
        keep = [buf[s, at:at + 8, :] for s in range(6)]
        upper = (keep[2] + keep[3]) + (keep[4] + keep[5])
        whole = upper + (keep[0] + keep[1])
        dst[0, at:at + 8, :] = upper
        dst[1, at:at + 8, :] = whole
        return whole

    def sparse_write(packed, chip, h):
        one, two = unpack(packed)
        for at, value in ((0, one), (HALF, two)):
            rows = pl.ds(pl.multiple_of(chip * LANES + at, HALF), HALF)
            xb[h, rows, :] = value[:HALF].astype(bf16)
        tail = pl.ds(pl.multiple_of(MAIN + chip * 16, 16), 16)
        xb[h, tail, :] = jnp.concatenate([one[HALF:], two[HALF:]], axis=0).astype(bf16)

    def sparse_block(buf, h):
        def each(chip):
            sparse_write(buf[chip, 0:BAND, :], chip, h)
        return each

    def sparse_dot(h):
        def rows_of(side):
            return dot(fsh[side], xb[h]) + dot(fsl[side], xb[h])
        return rows_of

    def combine_picks(inst, h, scalars):
        left_pack = low_lanes(BAND)

        def rows_of(side):
            got = dot(fssh[side], xb[h]) + dot(fssl[side], xb[h])
            got = got + swap(got)
            return jnp.where(left_pack, got[:BAND], got[BAND:])
        pps[inst, 0:BAND, :] = rows_of(1 - c)
        pps[inst, BAND:MSG, :] = scalars
        copy = remote(pps.at[inst], ppr.at[inst], psend.at[inst], precv.at[inst], sibling)
        copy.start()
        pending.append(copy)
        mine = rows_of(c)
        copy.wait_recv()
        return mine + ppr[inst, 0:BAND, :], scalars + ppr[inst, BAND:MSG, :]

    def add(first, second, scale):
        out = dict(first)
        for key, value in second.items():
            out[key] = out[key] + scale * value if key in out else scale * value
        return out

    def full_rows(inst, h, weights):
        for chip in range(CHIPS):
            value = None
            for g, weight in weights.items():
                term = weight * xg[g * 2 + h, chip, 0:BAND, :]
                value = term if value is None else value + term
            sparse_write(value, chip, h)
        return combine(inst, sparse_dot(h), zeros8)[0]

    zeros8 = jnp.zeros((8, LANES), f32)

    def inner_rows(residual, image):
        gamma = jnp.sum(own[...] * residual * residual, axis=0, keepdims=True)
        delta = jnp.sum(residual * image, axis=0, keepdims=True)
        return jnp.concatenate([gamma, delta, jnp.zeros((6, LANES), f32)], axis=0)

    def chain(h):
        along_wait(h, dense_block(cg.at[h], h))
        yield

        def part_of(yy, cc):
            side = yy * 2 + cc
            rows = cb[h, 0:4 * ROWS, :]
            got = dot(kh[side], rows) + dot(kl[side], rows)
            got = got + swap(got)
            return jnp.where(left, got[:LANES], got[LANES:])
        cps[h, 0:LANES, :] = part_of(1 - ylo, 1 - c)
        cps[h, LANES:, :] = part_of(ylo, 1 - c)
        copy = remote(cps.at[h], cpr.at[h], psend.at[h], precv.at[h], sibling)
        copy.start()
        pending.append(copy)
        away = part_of(1 - ylo, c)
        copy.wait_recv()
        yps[h] = away + cpr[h, 0:LANES, :]
        copy = remote(yps.at[h], ypr.at[h], ysend.at[h], yrecv.at[h], plane_dev(0, 1, 0))
        copy.start()
        pending.append(copy)
        here = part_of(ylo, c) + cpr[h, LANES:, :]
        yield
        copy.wait_recv()
        sg[h, q] = here + ypr[h]
        gather_start(sg.at[h], 2 + h)
        yield
        gather_wait(sg.at[h], 2 + h, dense_block(sg.at[h], h))
        yield
        total, _ = combine(2 + h, dense_dot(fhi, flo, h), zeros8)
        base[h] = total
        mine = pick_rows(total)
        scalars = zeros8
        gamma_was = alpha_was = None
        for g in range(ITERS + 1):
            e = g * 2 + h
            if g == ITERS:
                fw[h, len(COLUMN)] = scalars
                for k, (dz, fy) in enumerate(COLUMN):
                    copy = remote(fw.at[h, len(COLUMN)], fw.at[h, k], asend.at[h, k], arecv.at[h, k], column_dev(dz, fy))
                    copy.start()
                    pending.append(copy)
                yield
                tx[h] = full_rows(12 + 3 * h, h, wx)
                tr[h] = full_rows(13 + 3 * h, h, wr)
                tp[h] = full_rows(14 + 3 * h, h, wp)
                yield
                sums = scalars
                for k, (dz, fy) in enumerate(COLUMN):
                    here = fw.at[h, k]
                    remote(here, here, asend.at[h, k], arecv.at[h, k], column_dev(dz, fy)).wait_recv()
                    sums = sums + fw[h, k]
                fg[h, q] = sums
                gather_start(fg.at[h], 12 + h)
                yield
                gather_wait(fg.at[h], 12 + h, lambda chip: None)
                sums = zeros8
                for chip in range(CHIPS):
                    sums = sums + fg[h, chip]
                fps[h] = sums
                copy = remote(fps.at[h], fpr.at[h], psend.at[18 + h], precv.at[18 + h], sibling)
                copy.start()
                pending.append(copy)
                yield
                copy.wait_recv()
                sums = sums + fpr[h]
            else:
                buf = windows[h][g]
                buf[near_slot(0, 0), 0:BAND, :] = mine
                buf[near_slot(0, 0), BAND:MSG, :] = scalars
                near_start(buf, e)
                yield
                near_wait(buf, e)
                for t in range(2):
                    for b in range(3):
                        band = slice(b * SHARE, (b + 1) * SHARE)
                        far_s[e, t, band, :] = jnp.where(
                            left_band, buf[far_places[t][b], band, :], buf[far_places[t][b + 3], band, :])
                whole = sums_far(buf, far_s.at[e], BAND)
                far_start(far_s.at[e], far_r.at[e], e)
                yield
                far_wait(far_r.at[e], e)
                pieces = []
                for b in range(3):
                    band = slice(b * SHARE, (b + 1) * SHARE)
                    sides = []
                    for r in (b, b + 3):
                        rel, inside, slot = my_places[r]
                        away = jnp.where(rel < 5, far_r[e, 1, band, :], far_r[e, 0, band, :])
                        sides.append(jnp.where(inside, buf[slot, band, :], away))
                    pieces.append(mine[band, :] - jnp.where(left_band, sides[0], sides[1]))
                vector = jnp.concatenate(pieces, axis=0)
                xg[e, q, 0:BAND, :] = vector
                xg[e, q, BAND:MSG, :] = whole + far_r[e, 0, BAND:MSG, :] + far_r[e, 1, BAND:MSG, :]
                gather_start(xg.at[e], 4 + e)
                yield
                gather_wait(xg.at[e], 4 + e, sparse_block(xg.at[e], h))
                yield
                sums = zeros8
                for chip in range(CHIPS):
                    sums = sums + xg[e, chip, BAND:MSG, :]
                applied, sums = combine_picks(4 + e, h, sums)
            if g == 0:
                vr[h] = vector
                trp[h] = applied
                mine = applied
                scalars = inner_rows(vector, mine)
                wr = {0: jnp.ones((1, LANES), f32)}
                continue
            sums = sums + swap(sums)
            gamma, delta = sums[0:1], sums[1:2]
            residual = vr[h]
            if g == 1:
                alpha = gamma / delta
                step, direction, step_image = vector, residual, applied
                wp, ws = wr, {}
            else:
                beta = gamma / gamma_was
                alpha = gamma / (delta - beta * gamma / alpha_was)
                direction = residual + beta * vp[h]
                if g < ITERS:
                    step = vector + beta * vs[h]
                    step_image = applied + beta * tsp[h]
                    wp = add(wr, wp, beta)
                    ws = add({}, ws, beta)
            if g < ITERS:
                mine = trp[h] - alpha * step_image
                residual = residual - alpha * step
                scalars = inner_rows(residual, mine)
                ws[g] = jnp.ones((1, LANES), f32)
                wx = add(wx if g > 1 else {}, wp, alpha)
                wr = add(wr, ws, -alpha)
                vr[h] = residual
                vs[h] = step
                vp[h] = direction
                trp[h] = mine
                tsp[h] = step_image
                vx[h] = alpha * direction if g == 1 else vx[h] + alpha * direction
            else:
                vx[h] += alpha * direction
                base[h] = base[h] - (tx[h] + alpha * (tr[h] + beta * tp[h]))
            gamma_was, alpha_was = gamma, alpha

    chains = (chain(0), chain(1))

    def go(which):
        next(chains[which], None)

    for copy in flex_copies:
        copy.wait()
    for copy in shared_copies:
        copy.wait_recv()
    lax.fori_loop(0, 2 * CHIPS, split_flex, 0)
    go(0)
    go(0)
    go(1)
    go(0)
    go(1)
    pick_columns(0)
    go(1)
    pick_columns(1)
    for which in (0, 0, 1, 1, 0, 1, 0, 1, 0, 0, 1, 1):
        go(which)
    for _ in range(ITERS - 2):
        for which in (0, 1, 0, 1, 0, 0, 1, 1):
            go(which)
    for which in (0, 1, 0, 1, 0, 0, 0, 1, 1, 0, 1, 1, 0, 0, 1, 1):
        go(which)

    side = low_lanes(ROWS)
    trace_out[0] = jnp.where(side, base[0], base[1])
    for b in range(3):
        band = slice(b * SHARE, (b + 1) * SHARE)
        lower, upper = vx[0, band, :], vx[1, band, :]
        sign = sgn[band, :]
        lower, upper = sign * lower, sign * upper
        mult_out[0, b] = jnp.where(left_band, lower, swap(upper))
        mult_out[0, b + 3] = jnp.where(left_band, swap(lower), upper)

    for copy in pending:
        copy.wait_send()


def settle(mult, trace, mult_out, trace_out):
    mult_out[...] = mult[...]
    trace_out[...] = trace[...]


def body(edge_mid, edge_dir, seg_mid, seg_vec, currents, flexibility, partner, edge_block):
    vmem = pl.BlockSpec(memory_space=pltpu.VMEM)
    smem = pl.BlockSpec(memory_space=pltpu.SMEM)
    dma = pltpu.SemaphoreType.DMA
    half = CHIPS * ROWS

    def room(*shape):
        return pltpu.VMEM(shape, f32)

    def short(*shape):
        return pltpu.VMEM(shape, bf16)
    both = 2 * ITERS
    scratch = [
        room(4, 8, ROWS), room(4, 8, ROWS),
        room(2, 4, LANES, LANES),
        room(2, CHIPS, LANES, LANES),
        room(both, CHIPS, MSG, LANES),
        room(2, CHIPS, 8, LANES),
        room(18, LANES + 8, LANES), room(18, LANES + 8, LANES),
        room(12, MSG, LANES), room(12, MSG, LANES), room(2, 8, LANES), room(2, 8, LANES),
        room(2, 2 * LANES, LANES), room(2, 2 * LANES, LANES), room(2, LANES, LANES), room(2, LANES, LANES),
    ]
    scratch += [room(6, MSG, LANES)] * both
    scratch += [room(2, 16, 8, LANES), room(both, 2, MSG, LANES), room(both, 2, MSG, LANES)]
    scratch += [
        room(2, ROWS, half), short(2, ROWS, half), short(2, ROWS, half),
        short(2, ROWS, DEPTH), short(2, ROWS, DEPTH),
        short(2, PICKS, DEPTH), short(2, PICKS, DEPTH), room(2, ROWS, LANES),
        short(4, ROWS, 4 * ROWS), short(4, ROWS, 4 * ROWS),
        short(2, half, LANES), short(2, DEPTH, LANES),
        room(ROWS, ROWS), room(ROWS, ROWS), short(PICKS, ROWS), room(ROWS, ROWS),
        room(LANES, ROWS), room(4, 6, ROWS, LANES),
        room(BAND, LANES), room(BAND, LANES),
    ]
    scratch += [room(2, ROWS, LANES)] * 4
    scratch += [room(2, BAND, LANES)] * 6
    scratch += [
        dma((8,)), dma((8,)), dma((8,)), dma((3,)), dma((3,)), dma((3,)), dma((3,)),
        dma((14, 7)), dma((14, 7)), dma((20,)), dma((20,)), dma((2,)), dma((2,)),
        dma((8, 5)), dma((8, 5)), dma((8, 2)), dma((8, 2)), dma((2, 15)), dma((2, 15)),
    ]
    outs = (
        jax.ShapeDtypeStruct((1, ROUNDS, SHARE, LANES), f32),
        jax.ShapeDtypeStruct((1, ROWS, LANES), f32),
    )
    solved = pl.pallas_call(
        kernel,
        out_shape=outs,
        in_specs=[vmem] * 5 + [smem] * 2 + [pl.BlockSpec(memory_space=pl.ANY)],
        out_specs=(vmem, vmem),
        scratch_shapes=scratch,
        compiler_params=pltpu.CompilerParams(
            collective_id=0, has_side_effects=True, vmem_limit_bytes=56 * 1024 * 1024),
        name="interface_cg",
    )(jnp.transpose(edge_mid, (1, 0, 2)), jnp.transpose(edge_dir, (1, 0, 2)),
      seg_mid, seg_vec, currents, partner, edge_block, flexibility)
    return pl.pallas_call(
        settle,
        out_shape=outs,
        in_specs=[vmem] * 2,
        out_specs=(vmem, vmem),
        name="settle",
    )(*solved)


def solution(mesh):
    in_specs = (
        P("sub", None, "seg"),
        P("sub", None, "seg"),
        P(None, "seg"),
        P(None, "seg"),
        P(None, "seg"),
        P("sub", "seg", None),
        P(),
        P(None, "sub", None),
    )
    out_specs = (P("sub", None, "seg", None), P("sub", "seg", None))
    return jax.shard_map(body, mesh=mesh, in_specs=in_specs, out_specs=out_specs, check_vma=False)
```

```python
import jax
import jax.numpy as jnp
from jax import lax
from jax.experimental import pallas as pl
from jax.experimental.pallas import tpu as pltpu
from jax.sharding import PartitionSpec as P

ITERS = 4
ROUNDS = 6
SHARE = 24
PICKS = ROUNDS * SHARE
BAND = PICKS // 2
MSG = BAND + 8
ROWS = 256
LANES = 128
HALF = LANES // 2
CHIPS = 8
MAIN = CHIPS * LANES
DEPTH = CHIPS * PICKS
CORE2 = 0.05 * 0.05
f32 = jnp.float32
bf16 = jnp.bfloat16
MESH = pl.DeviceIdType.MESH

PLANE = ((0, 1), (1, 0), (-1, 0), (1, 1), (-1, 1), (2, 0), (2, 1))
ALONG = (1, -1, 2)
NEAR = ((0, 1), (1, 0), (-1, 0), (1, 1), (-1, 1))
FAR = (3, -3)
COLUMN = tuple((dz, fy) for dz in (4, -3, 3, -2, 2, -1, 1, 0) for fy in (1, 0) if dz or fy)


def split2(value):
    high = value.astype(bf16)
    return high, (value - high.astype(f32)).astype(bf16)


def dot(a, b):
    return jnp.dot(a, b, preferred_element_type=f32)


def kernel(em, ed, sm, sv, cur, part, eb, flex,
           mult_out, trace_out,
           geo, ge, cg, sg, xg, fg, ps, pr, pps, ppr, fps, fpr, cps, cpr, yps, ypr,
           wa0, wa1, wa2, wa3, wb0, wb1, wb2, wb3, fw, far_s, far_r,
           fv, fhi, flo, fsh, fsl, fssh, fssl, rem, kh, kl, cb, xb, pt, pk, ptb, pb, est, ebc,
           sgn, own, base, tx, tr, tp, trp, tsp, vr, vs, vp, vx,
           fsem, fsend, frecv, esend, erecv, gsend, grecv, dsend, drecv, psend, precv, ysend, yrecv,
           nsend, nrecv, zsend, zrecv, asend, arecv):
    seg = lax.axis_index("seg")
    sub = lax.axis_index("sub")
    x, ylo, c = seg // 4, (seg // 2) % 2, seg % 2
    z, yh = sub // 2, sub % 2
    q = seg // 2
    windows = ((wa0, wa1, wa2, wa3), (wb0, wb1, wb2, wb3))

    def plane_dev(dx, fy, fc):
        yy = 1 - ylo if fy else ylo
        cc = 1 - c if fc else c
        return (((x + dx + 4) % 4) * 4 + yy * 2 + cc, sub)

    def column_dev(dz, fy):
        yy = 1 - yh if fy else yh
        return (seg, ((z + dz + 8) % 8) * 2 + yy)

    def chip_from(dx, fy):
        yy = 1 - ylo if fy else ylo
        return ((x - dx + 4) % 4) * 2 + yy

    def remote(src, dst, ss, rs, dev):
        return pltpu.make_async_remote_copy(
            src_ref=src, dst_ref=dst, send_sem=ss, recv_sem=rs, device_id=dev, device_id_type=MESH)

    pending = []
    sibling = plane_dev(0, 0, 1)

    def low_lanes(rows):
        return lax.broadcasted_iota(jnp.int32, (rows, LANES), 1) < HALF

    def swap(value):
        return pltpu.roll(value, HALF, 1)

    flex_copies = []
    for chip in range(CHIPS):
        src = flex.at[0, :, pl.ds(pl.multiple_of((chip * 2 + c) * ROWS, ROWS), ROWS)]
        copy = pltpu.make_async_copy(src, fv.at[c, :, chip * ROWS:(chip + 1) * ROWS], fsem.at[chip])
        copy.start()
        flex_copies.append(copy)
    barrier = pltpu.get_barrier_semaphore()
    peers = [plane_dev(dx, fy, 0) for dx, fy in PLANE] + [sibling, plane_dev(0, 1, 1)]
    peers += [column_dev(dz, fy) for dz, fy in COLUMN]
    for peer in peers:
        pl.semaphore_signal(barrier, inc=1, device_id=peer, device_id_type=MESH)
    geo[x, 0:3, :] = sm[...]
    geo[x, 3:6, :] = sv[...]
    geo[x, 6:8, :] = jnp.zeros((2, ROWS), f32)
    my_set = ylo * 2 + c
    for comp in range(3):
        ge[my_set, comp:comp + 1, :] = em[comp]
        ge[my_set, 3 + comp:4 + comp, :] = ed[comp]
    ge[my_set, 6:8, :] = jnp.zeros((2, ROWS), f32)
    turned = cur[...].T
    left = low_lanes(LANES)
    cg[0, x] = jnp.where(left, turned[:LANES], swap(turned[LANES:]))
    cg[1, x] = jnp.where(left, swap(turned[:LANES]), turned[LANES:])
    pl.semaphore_wait(barrier, len(peers))

    edge_copies = []
    for k, (fy, fc) in enumerate(((0, 1), (1, 0), (1, 1))):
        copy = remote(ge.at[my_set], ge.at[my_set], esend.at[k], erecv.at[k], plane_dev(0, fy, fc))
        copy.start()
        edge_copies.append(copy)
    geo_copies = []
    for k, dx in enumerate(ALONG):
        copy = remote(geo.at[x], geo.at[x], gsend.at[k], grecv.at[k], plane_dev(dx, 0, 0))
        copy.start()
        geo_copies.append(copy)
    pending.extend(edge_copies + geo_copies)

    def along_start(h):
        for k, dx in enumerate(ALONG):
            copy = remote(cg.at[h, x], cg.at[h, x], dsend.at[h, k], drecv.at[h, k], plane_dev(dx, 0, 0))
            copy.start()
            pending.append(copy)

    def along_wait(h, each):
        each(x)
        for k, dx in enumerate(ALONG):
            origin = (x - dx + 4) % 4
            here = cg.at[h, origin]
            remote(here, here, dsend.at[h, k], drecv.at[h, k], sibling).wait_recv()
            each(origin)

    def gather_start(buf, g):
        mine = buf.at[q]
        for k, (dx, fy) in enumerate(PLANE):
            copy = remote(mine, mine, dsend.at[g, k], drecv.at[g, k], plane_dev(dx, fy, 0))
            copy.start()
            pending.append(copy)

    def gather_wait(buf, g, each):
        each(q)
        for k, (dx, fy) in enumerate(PLANE):
            origin = chip_from(dx, fy)
            here = buf.at[origin]
            remote(here, here, dsend.at[g, k], drecv.at[g, k], sibling).wait_recv()
            each(origin)

    along_start(0)
    along_start(1)
    shared_copies = []
    for chip in range(CHIPS):
        src = flex.at[0, :, pl.ds(pl.multiple_of((chip * 2 + 1 - c) * ROWS, ROWS), ROWS)]
        dst = fv.at[c, :, chip * ROWS:(chip + 1) * ROWS]
        copy = remote(src, dst, fsend.at[chip], frecv.at[chip], sibling)
        copy.start()
        shared_copies.append(copy)
    pending.extend(shared_copies)

    lane_at = lax.broadcasted_iota(jnp.int32, (1, ROWS), 1)
    pt[...] = jnp.zeros((ROWS, ROWS), f32)
    pk[...] = jnp.zeros((ROWS, ROWS), f32)

    def hot_row(k, carry):
        row = jnp.where(lane_at == eb[k // SHARE, 0, k % SHARE], 1.0, 0.0).astype(f32)
        upper = k // BAND
        at = k - upper * BAND
        place = jnp.where(at < HALF, upper * HALF + at, LANES + upper * 8 + at - HALF)
        pt[pl.ds(k, 1), :] = row
        pk[pl.ds(place, 1), :] = row
        return carry
    lax.fori_loop(0, PICKS, hot_row, 0)
    ptb[...] = pt[0:PICKS, :].astype(bf16)
    pb[...] = pk[...].T

    for copy in edge_copies:
        copy.wait_recv()
    for side in range(4):
        est[...] = jnp.zeros((LANES, ROWS), f32)
        est[0:8, :] = ge[side]
        columns = est[...].T
        for comp in range(6):
            ebc[side, comp] = jnp.broadcast_to(columns[:, comp:comp + 1], (ROWS, LANES))

    left_band = low_lanes(SHARE)
    for b in range(3):
        band = slice(b * SHARE, (b + 1) * SHARE)
        first = jnp.where(part[b, sub] > sub, 1.0, 0.0).astype(f32)
        second = jnp.where(part[b + 3, sub] > sub, 1.0, 0.0).astype(f32)
        mark = jnp.where(left_band, first, second)
        own[band, :] = mark
        sgn[band, :] = mark * 2.0 - 1.0

    for copy in geo_copies:
        copy.wait_recv()

    def tile(step, carry):
        side, chip = step // 4, step % 4
        for h in range(2):
            row = [geo[chip, pl.ds(comp, 1), h * LANES:(h + 1) * LANES] for comp in range(6)]
            lanes = pl.ds(pl.multiple_of(chip * ROWS + h * LANES, LANES), LANES)
            for part_at in range(4):
                rows = slice(part_at * 64, part_at * 64 + 64)
                dist = jnp.full((64, LANES), CORE2, f32)
                along = jnp.zeros((64, LANES), f32)
                for comp in range(3):
                    gap = ebc[side, comp, rows, :] - row[comp]
                    dist = dist + gap * gap
                    along = along + ebc[side, 3 + comp, rows, :] * row[3 + comp]
                high, low = split2(along * lax.rsqrt(dist))
                kh[side, rows, lanes] = high
                kl[side, rows, lanes] = low
        return carry
    lax.fori_loop(0, 16, tile, 0)

    def unpack(value):
        high = value.astype(bf16).astype(f32)
        low = value - high
        side = low_lanes(value.shape[0])
        return jnp.where(side, high, swap(low)), jnp.where(side, swap(high), low)

    def dense_block(buf, h):
        def each(chip):
            one, two = unpack(buf[chip])
            cb[h, pl.ds(pl.multiple_of(chip * ROWS, LANES), LANES), :] = one.astype(bf16)
            cb[h, pl.ds(pl.multiple_of(chip * ROWS + LANES, LANES), LANES), :] = two.astype(bf16)
        return each

    def dense_dot(high, low, h):
        def rows_of(side):
            return dot(high[side], cb[h]) + dot(low[side], cb[h])
        return rows_of

    def combine(inst, rows_of, scalars):
        other = rows_of(1 - c)
        other = other + swap(other)
        ps[inst, 0:LANES, :] = jnp.where(left, other[:LANES], other[LANES:])
        ps[inst, LANES:LANES + 8, :] = scalars
        copy = remote(ps.at[inst], pr.at[inst], psend.at[inst], precv.at[inst], sibling)
        copy.start()
        pending.append(copy)
        mine = rows_of(c)
        mine = mine + swap(mine)
        copy.wait_recv()
        got = pr[inst, 0:LANES, :]
        back = swap(got)
        top = mine[:LANES] + jnp.where(left, got, back)
        bottom = mine[LANES:] + jnp.where(left, back, got)
        return jnp.concatenate([top, bottom], axis=0), scalars + pr[inst, LANES:LANES + 8, :]

    def split_flex(step, carry):
        side, chip = step // CHIPS, step % CHIPS
        for h in range(2):
            lanes = pl.ds(pl.multiple_of(chip * ROWS + h * LANES, LANES), LANES)
            high, low = split2(fv[side, :, lanes])
            fhi[side, :, lanes] = high
            flo[side, :, lanes] = low
        return carry

    def pick_columns(half):
        rem[...] = jnp.zeros((2, ROWS, LANES), f32)

        def one(chip, carry):
            tail = pltpu.roll(pb[:, LANES:], chip * (PICKS - LANES), 1)
            choose = jnp.concatenate([pb[:, :LANES], tail], axis=1).astype(bf16)
            src = pl.ds(pl.multiple_of(chip * ROWS, ROWS), ROWS)
            dst = pl.ds(pl.multiple_of(chip * LANES, LANES), LANES)
            for at, (whole, out) in enumerate(((fhi, fsh), (flo, fsl))):
                got = dot(whole[half, :, src], choose)
                out[half, :, dst] = got[:, :LANES].astype(bf16)
                rem[at] += got[:, LANES:]
            return carry
        lax.fori_loop(0, CHIPS, one, 0)
        fsh[half, :, MAIN:] = rem[0].astype(bf16)
        fsl[half, :, MAIN:] = rem[1].astype(bf16)
        fssh[half] = dot(ptb[...], fsh[half]).astype(bf16)
        fssl[half] = dot(ptb[...], fsl[half]).astype(bf16)

    def pick_rows(full):
        high = full.astype(bf16)
        rest = full - high.astype(f32)
        mid = rest.astype(bf16)
        low = (rest - mid.astype(f32)).astype(bf16)
        both = dot(ptb[...], jnp.where(low_lanes(ROWS), high.astype(f32), mid.astype(f32)).astype(bf16))
        picked = (both + swap(both)) + dot(ptb[...], low)
        return jnp.where(low_lanes(BAND), picked[:BAND], picked[BAND:])

    def near_slot(dz, fy):
        return (dz + 1) * 2 + fy

    def near_start(buf, e):
        mine = buf.at[near_slot(0, 0)]
        for k, (dz, fy) in enumerate(NEAR):
            copy = remote(mine, buf.at[near_slot(-dz, fy)], nsend.at[e, k], nrecv.at[e, k], column_dev(dz, fy))
            copy.start()
            pending.append(copy)

    def near_wait(buf, e):
        for k, (dz, fy) in enumerate(NEAR):
            here = buf.at[near_slot(-dz, fy)]
            remote(here, here, nsend.at[e, k], nrecv.at[e, k], column_dev(dz, fy)).wait_recv()

    def far_start(src, dst, e):
        for t, dz in enumerate(FAR):
            copy = remote(src.at[t], dst.at[t], zsend.at[e, t], zrecv.at[e, t], column_dev(dz, 0))
            copy.start()
            pending.append(copy)

    def far_wait(dst, e):
        for t, dz in enumerate(FAR):
            here = dst.at[t]
            remote(here, here, zsend.at[e, t], zrecv.at[e, t], column_dev(dz, 0)).wait_recv()

    def place_of(r, at):
        p = part[r, at]
        rel = (p // 2 - z + 8) % 8
        shifted = (rel + 1) % 8
        slot = shifted * 2 + jnp.where(p % 2 == yh, 0, 1)
        inside = shifted < 3
        return rel, inside, jnp.where(inside, slot, 0)

    far_places = [[place_of(r, ((z + dz + 8) % 8) * 2 + yh)[2] for r in range(ROUNDS)] for dz in FAR]
    my_places = [place_of(r, sub) for r in range(ROUNDS)]

    def sums_far(buf, dst, at):
        keep = [buf[s, at:at + 8, :] for s in range(6)]
        upper = (keep[2] + keep[3]) + (keep[4] + keep[5])
        whole = upper + (keep[0] + keep[1])
        dst[0, at:at + 8, :] = upper
        dst[1, at:at + 8, :] = whole
        return whole

    def sparse_write(packed, chip, h):
        one, two = unpack(packed)
        for at, value in ((0, one), (HALF, two)):
            rows = pl.ds(pl.multiple_of(chip * LANES + at, HALF), HALF)
            xb[h, rows, :] = value[:HALF].astype(bf16)
        tail = pl.ds(pl.multiple_of(MAIN + chip * 16, 16), 16)
        xb[h, tail, :] = jnp.concatenate([one[HALF:], two[HALF:]], axis=0).astype(bf16)

    def sparse_block(buf, h):
        def each(chip):
            sparse_write(buf[chip, 0:BAND, :], chip, h)
        return each

    def sparse_dot(h):
        def rows_of(side):
            return dot(fsh[side], xb[h]) + dot(fsl[side], xb[h])
        return rows_of

    def combine_picks(inst, h, scalars):
        left_pack = low_lanes(BAND)

        def rows_of(side):
            got = dot(fssh[side], xb[h]) + dot(fssl[side], xb[h])
            got = got + swap(got)
            return jnp.where(left_pack, got[:BAND], got[BAND:])
        pps[inst, 0:BAND, :] = rows_of(1 - c)
        pps[inst, BAND:MSG, :] = scalars
        copy = remote(pps.at[inst], ppr.at[inst], psend.at[inst], precv.at[inst], sibling)
        copy.start()
        pending.append(copy)
        mine = rows_of(c)
        copy.wait_recv()
        return mine + ppr[inst, 0:BAND, :], scalars + ppr[inst, BAND:MSG, :]

    def add(first, second, scale):
        out = dict(first)
        for key, value in second.items():
            out[key] = out[key] + scale * value if key in out else scale * value
        return out

    def full_rows(inst, h, weights):
        for chip in range(CHIPS):
            value = None
            for g, weight in weights.items():
                term = weight * xg[g * 2 + h, chip, 0:BAND, :]
                value = term if value is None else value + term
            sparse_write(value, chip, h)
        return combine(inst, sparse_dot(h), zeros8)[0]

    zeros8 = jnp.zeros((8, LANES), f32)

    def inner_rows(residual, image):
        gamma = jnp.sum(own[...] * residual * residual, axis=0, keepdims=True)
        delta = jnp.sum(residual * image, axis=0, keepdims=True)
        return jnp.concatenate([gamma, delta, jnp.zeros((6, LANES), f32)], axis=0)

    def chain(h):
        along_wait(h, dense_block(cg.at[h], h))
        yield

        def part_of(yy, cc):
            side = yy * 2 + cc
            rows = cb[h, 0:4 * ROWS, :]
            got = dot(kh[side], rows) + dot(kl[side], rows)
            got = got + swap(got)
            return jnp.where(left, got[:LANES], got[LANES:])
        cps[h, 0:LANES, :] = part_of(1 - ylo, 1 - c)
        cps[h, LANES:, :] = part_of(ylo, 1 - c)
        copy = remote(cps.at[h], cpr.at[h], psend.at[h], precv.at[h], sibling)
        copy.start()
        pending.append(copy)
        away = part_of(1 - ylo, c)
        copy.wait_recv()
        yps[h] = away + cpr[h, 0:LANES, :]
        copy = remote(yps.at[h], ypr.at[h], ysend.at[h], yrecv.at[h], plane_dev(0, 1, 0))
        copy.start()
        pending.append(copy)
        here = part_of(ylo, c) + cpr[h, LANES:, :]
        yield
        copy.wait_recv()
        sg[h, q] = here + ypr[h]
        gather_start(sg.at[h], 2 + h)
        yield
        gather_wait(sg.at[h], 2 + h, dense_block(sg.at[h], h))
        yield
        total, _ = combine(2 + h, dense_dot(fhi, flo, h), zeros8)
        base[h] = total
        mine = pick_rows(total)
        scalars = zeros8
        gamma_was = alpha_was = None
        for g in range(ITERS + 1):
            e = g * 2 + h
            if g == ITERS:
                fw[h, len(COLUMN)] = scalars
                for k, (dz, fy) in enumerate(COLUMN):
                    copy = remote(fw.at[h, len(COLUMN)], fw.at[h, k], asend.at[h, k], arecv.at[h, k], column_dev(dz, fy))
                    copy.start()
                    pending.append(copy)
                yield
                tx[h] = full_rows(12 + 3 * h, h, wx)
                tr[h] = full_rows(13 + 3 * h, h, wr)
                tp[h] = full_rows(14 + 3 * h, h, wp)
                yield
                sums = scalars
                for k, (dz, fy) in enumerate(COLUMN):
                    here = fw.at[h, k]
                    remote(here, here, asend.at[h, k], arecv.at[h, k], column_dev(dz, fy)).wait_recv()
                    sums = sums + fw[h, k]
                fg[h, q] = sums
                gather_start(fg.at[h], 12 + h)
                yield
                gather_wait(fg.at[h], 12 + h, lambda chip: None)
                sums = zeros8
                for chip in range(CHIPS):
                    sums = sums + fg[h, chip]
                fps[h] = sums
                copy = remote(fps.at[h], fpr.at[h], psend.at[18 + h], precv.at[18 + h], sibling)
                copy.start()
                pending.append(copy)
                yield
                copy.wait_recv()
                sums = sums + fpr[h]
            else:
                buf = windows[h][g]
                buf[near_slot(0, 0), 0:BAND, :] = mine
                buf[near_slot(0, 0), BAND:MSG, :] = scalars
                near_start(buf, e)
                yield
                near_wait(buf, e)
                for t in range(2):
                    for b in range(3):
                        band = slice(b * SHARE, (b + 1) * SHARE)
                        far_s[e, t, band, :] = jnp.where(
                            left_band, buf[far_places[t][b], band, :], buf[far_places[t][b + 3], band, :])
                whole = sums_far(buf, far_s.at[e], BAND)
                far_start(far_s.at[e], far_r.at[e], e)
                yield
                far_wait(far_r.at[e], e)
                pieces = []
                for b in range(3):
                    band = slice(b * SHARE, (b + 1) * SHARE)
                    sides = []
                    for r in (b, b + 3):
                        rel, inside, slot = my_places[r]
                        away = jnp.where(rel < 5, far_r[e, 1, band, :], far_r[e, 0, band, :])
                        sides.append(jnp.where(inside, buf[slot, band, :], away))
                    pieces.append(mine[band, :] - jnp.where(left_band, sides[0], sides[1]))
                vector = jnp.concatenate(pieces, axis=0)
                xg[e, q, 0:BAND, :] = vector
                xg[e, q, BAND:MSG, :] = whole + far_r[e, 0, BAND:MSG, :] + far_r[e, 1, BAND:MSG, :]
                gather_start(xg.at[e], 4 + e)
                yield
                gather_wait(xg.at[e], 4 + e, sparse_block(xg.at[e], h))
                yield
                sums = zeros8
                for chip in range(CHIPS):
                    sums = sums + xg[e, chip, BAND:MSG, :]
                applied, sums = combine_picks(4 + e, h, sums)
            if g == 0:
                vr[h] = vector
                trp[h] = applied
                mine = applied
                scalars = inner_rows(vector, mine)
                wr = {0: jnp.ones((1, LANES), f32)}
                continue
            sums = sums + swap(sums)
            gamma, delta = sums[0:1], sums[1:2]
            residual = vr[h]
            if g == 1:
                alpha = gamma / delta
                step, direction, step_image = vector, residual, applied
                wp, ws = wr, {}
            else:
                beta = gamma / gamma_was
                alpha = gamma / (delta - beta * gamma / alpha_was)
                direction = residual + beta * vp[h]
                if g < ITERS:
                    step = vector + beta * vs[h]
                    step_image = applied + beta * tsp[h]
                    wp = add(wr, wp, beta)
                    ws = add({}, ws, beta)
            if g < ITERS:
                mine = trp[h] - alpha * step_image
                residual = residual - alpha * step
                scalars = inner_rows(residual, mine)
                ws[g] = jnp.ones((1, LANES), f32)
                wx = add(wx if g > 1 else {}, wp, alpha)
                wr = add(wr, ws, -alpha)
                vr[h] = residual
                vs[h] = step
                vp[h] = direction
                trp[h] = mine
                tsp[h] = step_image
                vx[h] = alpha * direction if g == 1 else vx[h] + alpha * direction
            else:
                vx[h] += alpha * direction
                base[h] = base[h] - (tx[h] + alpha * (tr[h] + beta * tp[h]))
            gamma_was, alpha_was = gamma, alpha

    chains = (chain(0), chain(1))

    def go(which):
        next(chains[which], None)

    for copy in flex_copies:
        copy.wait()
    for copy in shared_copies:
        copy.wait_recv()
    lax.fori_loop(0, 2 * CHIPS, split_flex, 0)
    go(0)
    go(0)
    go(1)
    go(0)
    go(1)
    pick_columns(0)
    go(1)
    pick_columns(1)
    turn = (0, 0, 1, 1, 0, 0, 1, 1)
    for which in (0, 0, 1, 1) + turn * (ITERS - 1) + (0, 0, 1, 1, 0, 0, 0, 1, 1, 0, 1, 1, 0, 0, 1, 1):
        go(which)

    side = low_lanes(ROWS)
    trace_out[0] = jnp.where(side, base[0], base[1])
    for b in range(3):
        band = slice(b * SHARE, (b + 1) * SHARE)
        lower, upper = vx[0, band, :], vx[1, band, :]
        sign = sgn[band, :]
        lower, upper = sign * lower, sign * upper
        mult_out[0, b] = jnp.where(left_band, lower, swap(upper))
        mult_out[0, b + 3] = jnp.where(left_band, swap(lower), upper)

    for copy in pending:
        copy.wait_send()


def settle(mult, trace, mult_out, trace_out):
    mult_out[...] = mult[...]
    trace_out[...] = trace[...]


def body(edge_mid, edge_dir, seg_mid, seg_vec, currents, flexibility, partner, edge_block):
    vmem = pl.BlockSpec(memory_space=pltpu.VMEM)
    smem = pl.BlockSpec(memory_space=pltpu.SMEM)
    dma = pltpu.SemaphoreType.DMA
    half = CHIPS * ROWS

    def room(*shape):
        return pltpu.VMEM(shape, f32)

    def short(*shape):
        return pltpu.VMEM(shape, bf16)
    both = 2 * ITERS
    scratch = [
        room(4, 8, ROWS), room(4, 8, ROWS),
        room(2, 4, LANES, LANES),
        room(2, CHIPS, LANES, LANES),
        room(both, CHIPS, MSG, LANES),
        room(2, CHIPS, 8, LANES),
        room(18, LANES + 8, LANES), room(18, LANES + 8, LANES),
        room(12, MSG, LANES), room(12, MSG, LANES), room(2, 8, LANES), room(2, 8, LANES),
        room(2, 2 * LANES, LANES), room(2, 2 * LANES, LANES), room(2, LANES, LANES), room(2, LANES, LANES),
    ]
    scratch += [room(6, MSG, LANES)] * both
    scratch += [room(2, 16, 8, LANES), room(both, 2, MSG, LANES), room(both, 2, MSG, LANES)]
    scratch += [
        room(2, ROWS, half), short(2, ROWS, half), short(2, ROWS, half),
        short(2, ROWS, DEPTH), short(2, ROWS, DEPTH),
        short(2, PICKS, DEPTH), short(2, PICKS, DEPTH), room(2, ROWS, LANES),
        short(4, ROWS, 4 * ROWS), short(4, ROWS, 4 * ROWS),
        short(2, half, LANES), short(2, DEPTH, LANES),
        room(ROWS, ROWS), room(ROWS, ROWS), short(PICKS, ROWS), room(ROWS, ROWS),
        room(LANES, ROWS), room(4, 6, ROWS, LANES),
        room(BAND, LANES), room(BAND, LANES),
    ]
    scratch += [room(2, ROWS, LANES)] * 4
    scratch += [room(2, BAND, LANES)] * 6
    scratch += [
        dma((8,)), dma((8,)), dma((8,)), dma((3,)), dma((3,)), dma((3,)), dma((3,)),
        dma((14, 7)), dma((14, 7)), dma((20,)), dma((20,)), dma((2,)), dma((2,)),
        dma((8, 5)), dma((8, 5)), dma((8, 2)), dma((8, 2)), dma((2, 15)), dma((2, 15)),
    ]
    outs = (
        jax.ShapeDtypeStruct((1, ROUNDS, SHARE, LANES), f32),
        jax.ShapeDtypeStruct((1, ROWS, LANES), f32),
    )
    solved = pl.pallas_call(
        kernel,
        out_shape=outs,
        in_specs=[vmem] * 5 + [smem] * 2 + [pl.BlockSpec(memory_space=pl.ANY)],
        out_specs=(vmem, vmem),
        scratch_shapes=scratch,
        compiler_params=pltpu.CompilerParams(
            collective_id=0, has_side_effects=True, vmem_limit_bytes=56 * 1024 * 1024),
        name="interface_cg",
    )(jnp.transpose(edge_mid, (1, 0, 2)), jnp.transpose(edge_dir, (1, 0, 2)),
      seg_mid, seg_vec, currents, partner, edge_block, flexibility)
    return pl.pallas_call(
        settle,
        out_shape=outs,
        in_specs=[vmem] * 2,
        out_specs=(vmem, vmem),
        name="settle",
    )(*solved)


def solution(mesh):
    in_specs = (
        P("sub", None, "seg"),
        P("sub", None, "seg"),
        P(None, "seg"),
        P(None, "seg"),
        P(None, "seg"),
        P("sub", "seg", None),
        P(),
        P(None, "sub", None),
    )
    out_specs = (P("sub", None, "seg", None), P("sub", "seg", None))
    return jax.shard_map(body, mesh=mesh, in_specs=in_specs, out_specs=out_specs, check_vma=False)
```

```python
import jax
import jax.numpy as jnp
from jax import lax
from jax.experimental import pallas as pl
from jax.experimental.pallas import tpu as pltpu
from jax.sharding import PartitionSpec as P

ITERS = 4
ROUNDS = 6
SHARE = 24
PICKS = ROUNDS * SHARE
BAND = PICKS // 2
MSG = BAND + 8
ROWS = 256
LANES = 128
HALF = LANES // 2
CHIPS = 8
MAIN = CHIPS * LANES
DEPTH = CHIPS * PICKS
CORE2 = 0.05 * 0.05
f32 = jnp.float32
bf16 = jnp.bfloat16
MESH = pl.DeviceIdType.MESH

PLANE = ((2, 1), (1, 1), (-1, 1), (2, 0), (1, 0), (-1, 0), (0, 1))
NEAR = ((0, 1), (1, 0), (-1, 0), (1, 1), (-1, 1))
FAR = (3, -3)
COLUMN = tuple((dz, fy) for dz in (4, -3, 3, -2, 2, -1, 1, 0) for fy in (1, 0) if dz or fy)


def split2(value):
    high = value.astype(bf16)
    return high, (value - high.astype(f32)).astype(bf16)


def dot(a, b):
    return jnp.dot(a, b, preferred_element_type=f32)


def kernel(em, ed, sm, sv, cur, part, eb, flex,
           mult_out, trace_out,
           geo, ge, cg, sg, xg, fg, ps, pr, pps, ppr, fps, fpr,
           wa0, wa1, wa2, wa3, wb0, wb1, wb2, wb3, fw, far_s, far_r,
           fv, fhi, flo, fsh, fsl, fssh, fssl, rem, kh, kl, cb, xb, pt, pk, ptb, pb, est, ebc,
           sgn, own, base, tx, tr, tp, trp, tsp, vr, vs, vp, vx,
           fsem, fsend, frecv, esend, erecv, gsend, grecv, dsend, drecv, psend, precv,
           nsend, nrecv, zsend, zrecv, asend, arecv):
    seg = lax.axis_index("seg")
    sub = lax.axis_index("sub")
    x, ylo, c = seg // 4, (seg // 2) % 2, seg % 2
    z, yh = sub // 2, sub % 2
    q = seg // 2
    windows = ((wa0, wa1, wa2, wa3), (wb0, wb1, wb2, wb3))

    def plane_dev(dx, fy, fc):
        yy = 1 - ylo if fy else ylo
        cc = 1 - c if fc else c
        return (((x + dx + 4) % 4) * 4 + yy * 2 + cc, sub)

    def column_dev(dz, fy):
        yy = 1 - yh if fy else yh
        return (seg, ((z + dz + 8) % 8) * 2 + yy)

    def chip_from(dx, fy):
        yy = 1 - ylo if fy else ylo
        return ((x - dx + 4) % 4) * 2 + yy

    def remote(src, dst, ss, rs, dev):
        return pltpu.make_async_remote_copy(
            src_ref=src, dst_ref=dst, send_sem=ss, recv_sem=rs, device_id=dev, device_id_type=MESH)

    pending = []
    sibling = plane_dev(0, 0, 1)

    def low_lanes(rows):
        return lax.broadcasted_iota(jnp.int32, (rows, LANES), 1) < HALF

    def swap(value):
        return pltpu.roll(value, HALF, 1)

    flex_copies = []
    for chip in range(CHIPS):
        src = flex.at[0, :, pl.ds(pl.multiple_of((chip * 2 + c) * ROWS, ROWS), ROWS)]
        copy = pltpu.make_async_copy(src, fv.at[c, :, chip * ROWS:(chip + 1) * ROWS], fsem.at[chip])
        copy.start()
        flex_copies.append(copy)
    barrier = pltpu.get_barrier_semaphore()
    peers = [plane_dev(dx, fy, 0) for dx, fy in PLANE] + [sibling]
    peers += [column_dev(dz, fy) for dz, fy in COLUMN]
    for peer in peers:
        pl.semaphore_signal(barrier, inc=1, device_id=peer, device_id_type=MESH)
    geo[q, 0:3, :] = sm[...]
    geo[q, 3:6, :] = sv[...]
    geo[q, 6:8, :] = jnp.zeros((2, ROWS), f32)
    for comp in range(3):
        ge[c, comp:comp + 1, :] = em[comp]
        ge[c, 3 + comp:4 + comp, :] = ed[comp]
    ge[c, 6:8, :] = jnp.zeros((2, ROWS), f32)
    turned = cur[...].T
    left = low_lanes(LANES)
    cg[0, q] = jnp.where(left, turned[:LANES], swap(turned[LANES:]))
    cg[1, q] = jnp.where(left, swap(turned[:LANES]), turned[LANES:])
    pl.semaphore_wait(barrier, len(peers))

    edge_copy = remote(ge.at[c], ge.at[c], esend, erecv, sibling)
    edge_copy.start()
    pending.append(edge_copy)
    geo_copies = []
    for k, (dx, fy) in enumerate(PLANE):
        copy = remote(geo.at[q], geo.at[q], gsend.at[k], grecv.at[k], plane_dev(dx, fy, 0))
        copy.start()
        geo_copies.append(copy)
    pending.extend(geo_copies)

    def gather_start(buf, g):
        mine = buf.at[q]
        for k, (dx, fy) in enumerate(PLANE):
            copy = remote(mine, mine, dsend.at[g, k], drecv.at[g, k], plane_dev(dx, fy, 0))
            copy.start()
            pending.append(copy)

    def gather_wait(buf, g, each):
        each(q)
        for k, (dx, fy) in enumerate(PLANE):
            origin = chip_from(dx, fy)
            here = buf.at[origin]
            remote(here, here, dsend.at[g, k], drecv.at[g, k], sibling).wait_recv()
            each(origin)

    gather_start(cg.at[0], 0)
    gather_start(cg.at[1], 1)
    shared_copies = []
    for chip in range(CHIPS):
        src = flex.at[0, :, pl.ds(pl.multiple_of((chip * 2 + 1 - c) * ROWS, ROWS), ROWS)]
        dst = fv.at[c, :, chip * ROWS:(chip + 1) * ROWS]
        copy = remote(src, dst, fsend.at[chip], frecv.at[chip], sibling)
        copy.start()
        shared_copies.append(copy)
    pending.extend(shared_copies)

    lane_at = lax.broadcasted_iota(jnp.int32, (1, ROWS), 1)
    pt[...] = jnp.zeros((ROWS, ROWS), f32)
    pk[...] = jnp.zeros((ROWS, ROWS), f32)

    def hot_row(k, carry):
        row = jnp.where(lane_at == eb[k // SHARE, 0, k % SHARE], 1.0, 0.0).astype(f32)
        upper = k // BAND
        at = k - upper * BAND
        place = jnp.where(at < HALF, upper * HALF + at, LANES + upper * 8 + at - HALF)
        pt[pl.ds(k, 1), :] = row
        pk[pl.ds(place, 1), :] = row
        return carry
    lax.fori_loop(0, PICKS, hot_row, 0)
    ptb[...] = pt[0:PICKS, :].astype(bf16)
    pb[...] = pk[...].T

    edge_copy.wait_recv()
    for side in range(2):
        est[...] = jnp.zeros((LANES, ROWS), f32)
        est[0:8, :] = ge[side]
        columns = est[...].T
        for comp in range(6):
            ebc[side, comp] = jnp.broadcast_to(columns[:, comp:comp + 1], (ROWS, LANES))

    left_band = low_lanes(SHARE)
    for b in range(3):
        band = slice(b * SHARE, (b + 1) * SHARE)
        first = jnp.where(part[b, sub] > sub, 1.0, 0.0).astype(f32)
        second = jnp.where(part[b + 3, sub] > sub, 1.0, 0.0).astype(f32)
        mark = jnp.where(left_band, first, second)
        own[band, :] = mark
        sgn[band, :] = mark * 2.0 - 1.0

    for copy in geo_copies:
        copy.wait_recv()

    def tile(step, carry):
        side, chip = step // CHIPS, step % CHIPS
        for h in range(2):
            row = [geo[chip, pl.ds(comp, 1), h * LANES:(h + 1) * LANES] for comp in range(6)]
            lanes = pl.ds(pl.multiple_of(chip * ROWS + h * LANES, LANES), LANES)
            for part_at in range(4):
                rows = slice(part_at * 64, part_at * 64 + 64)
                dist = jnp.full((64, LANES), CORE2, f32)
                along = jnp.zeros((64, LANES), f32)
                for comp in range(3):
                    gap = ebc[side, comp, rows, :] - row[comp]
                    dist = dist + gap * gap
                    along = along + ebc[side, 3 + comp, rows, :] * row[3 + comp]
                high, low = split2(along * lax.rsqrt(dist))
                kh[side, rows, lanes] = high
                kl[side, rows, lanes] = low
        return carry
    lax.fori_loop(0, 2 * CHIPS, tile, 0)

    def unpack(value):
        high = value.astype(bf16).astype(f32)
        low = value - high
        side = low_lanes(value.shape[0])
        return jnp.where(side, high, swap(low)), jnp.where(side, swap(high), low)

    def dense_block(buf, h):
        def each(chip):
            one, two = unpack(buf[chip])
            cb[h, pl.ds(pl.multiple_of(chip * ROWS, LANES), LANES), :] = one.astype(bf16)
            cb[h, pl.ds(pl.multiple_of(chip * ROWS + LANES, LANES), LANES), :] = two.astype(bf16)
        return each

    def dense_dot(high, low, h):
        def rows_of(side):
            return dot(high[side], cb[h]) + dot(low[side], cb[h])
        return rows_of

    def combine(inst, rows_of, scalars):
        other = rows_of(1 - c)
        other = other + swap(other)
        ps[inst, 0:LANES, :] = jnp.where(left, other[:LANES], other[LANES:])
        ps[inst, LANES:LANES + 8, :] = scalars
        copy = remote(ps.at[inst], pr.at[inst], psend.at[inst], precv.at[inst], sibling)
        copy.start()
        pending.append(copy)
        mine = rows_of(c)
        mine = mine + swap(mine)
        copy.wait_recv()
        got = pr[inst, 0:LANES, :]
        back = swap(got)
        top = mine[:LANES] + jnp.where(left, got, back)
        bottom = mine[LANES:] + jnp.where(left, back, got)
        return jnp.concatenate([top, bottom], axis=0), scalars + pr[inst, LANES:LANES + 8, :]

    def split_flex(step, carry):
        side, chip = step // CHIPS, step % CHIPS
        for h in range(2):
            lanes = pl.ds(pl.multiple_of(chip * ROWS + h * LANES, LANES), LANES)
            high, low = split2(fv[side, :, lanes])
            fhi[side, :, lanes] = high
            flo[side, :, lanes] = low
        return carry

    def pick_columns(half):
        rem[...] = jnp.zeros((2, ROWS, LANES), f32)

        def one(chip, carry):
            tail = pltpu.roll(pb[:, LANES:], chip * (PICKS - LANES), 1)
            choose = jnp.concatenate([pb[:, :LANES], tail], axis=1).astype(bf16)
            src = pl.ds(pl.multiple_of(chip * ROWS, ROWS), ROWS)
            dst = pl.ds(pl.multiple_of(chip * LANES, LANES), LANES)
            for at, (whole, out) in enumerate(((fhi, fsh), (flo, fsl))):
                got = dot(whole[half, :, src], choose)
                out[half, :, dst] = got[:, :LANES].astype(bf16)
                rem[at] += got[:, LANES:]
            return carry
        lax.fori_loop(0, CHIPS, one, 0)
        fsh[half, :, MAIN:] = rem[0].astype(bf16)
        fsl[half, :, MAIN:] = rem[1].astype(bf16)
        fssh[half] = dot(ptb[...], fsh[half]).astype(bf16)
        fssl[half] = dot(ptb[...], fsl[half]).astype(bf16)

    def pick_rows(full):
        high = full.astype(bf16)
        rest = full - high.astype(f32)
        mid = rest.astype(bf16)
        low = (rest - mid.astype(f32)).astype(bf16)
        both = dot(ptb[...], jnp.where(low_lanes(ROWS), high.astype(f32), mid.astype(f32)).astype(bf16))
        picked = (both + swap(both)) + dot(ptb[...], low)
        return jnp.where(low_lanes(BAND), picked[:BAND], picked[BAND:])

    def near_slot(dz, fy):
        return (dz + 1) * 2 + fy

    def near_start(buf, e):
        mine = buf.at[near_slot(0, 0)]
        for k, (dz, fy) in enumerate(NEAR):
            copy = remote(mine, buf.at[near_slot(-dz, fy)], nsend.at[e, k], nrecv.at[e, k], column_dev(dz, fy))
            copy.start()
            pending.append(copy)

    def near_wait(buf, e):
        for k, (dz, fy) in enumerate(NEAR):
            here = buf.at[near_slot(-dz, fy)]
            remote(here, here, nsend.at[e, k], nrecv.at[e, k], column_dev(dz, fy)).wait_recv()

    def far_start(src, dst, e):
        for t, dz in enumerate(FAR):
            copy = remote(src.at[t], dst.at[t], zsend.at[e, t], zrecv.at[e, t], column_dev(dz, 0))
            copy.start()
            pending.append(copy)

    def far_wait(dst, e):
        for t, dz in enumerate(FAR):
            here = dst.at[t]
            remote(here, here, zsend.at[e, t], zrecv.at[e, t], column_dev(dz, 0)).wait_recv()

    def place_of(r, at):
        p = part[r, at]
        rel = (p // 2 - z + 8) % 8
        shifted = (rel + 1) % 8
        slot = shifted * 2 + jnp.where(p % 2 == yh, 0, 1)
        inside = shifted < 3
        return rel, inside, jnp.where(inside, slot, 0)

    far_places = [[place_of(r, ((z + dz + 8) % 8) * 2 + yh)[2] for r in range(ROUNDS)] for dz in FAR]
    my_places = [place_of(r, sub) for r in range(ROUNDS)]

    def sums_far(buf, dst, at):
        keep = [buf[s, at:at + 8, :] for s in range(6)]
        upper = (keep[2] + keep[3]) + (keep[4] + keep[5])
        whole = upper + (keep[0] + keep[1])
        dst[0, at:at + 8, :] = upper
        dst[1, at:at + 8, :] = whole
        return whole

    def sparse_write(packed, chip, h):
        one, two = unpack(packed)
        for at, value in ((0, one), (HALF, two)):
            rows = pl.ds(pl.multiple_of(chip * LANES + at, HALF), HALF)
            xb[h, rows, :] = value[:HALF].astype(bf16)
        tail = pl.ds(pl.multiple_of(MAIN + chip * 16, 16), 16)
        xb[h, tail, :] = jnp.concatenate([one[HALF:], two[HALF:]], axis=0).astype(bf16)

    def sparse_block(buf, h):
        def each(chip):
            sparse_write(buf[chip, 0:BAND, :], chip, h)
        return each

    def sparse_dot(h):
        def rows_of(side):
            return dot(fsh[side], xb[h]) + dot(fsl[side], xb[h])
        return rows_of

    def combine_picks(inst, h, scalars):
        left_pack = low_lanes(BAND)

        def rows_of(side):
            got = dot(fssh[side], xb[h]) + dot(fssl[side], xb[h])
            got = got + swap(got)
            return jnp.where(left_pack, got[:BAND], got[BAND:])
        pps[inst, 0:BAND, :] = rows_of(1 - c)
        pps[inst, BAND:MSG, :] = scalars
        copy = remote(pps.at[inst], ppr.at[inst], psend.at[inst], precv.at[inst], sibling)
        copy.start()
        pending.append(copy)
        mine = rows_of(c)
        copy.wait_recv()
        return mine + ppr[inst, 0:BAND, :], scalars + ppr[inst, BAND:MSG, :]

    def add(first, second, scale):
        out = dict(first)
        for key, value in second.items():
            out[key] = out[key] + scale * value if key in out else scale * value
        return out

    def full_rows(inst, h, weights):
        for chip in range(CHIPS):
            value = None
            for g, weight in weights.items():
                term = weight * xg[g * 2 + h, chip, 0:BAND, :]
                value = term if value is None else value + term
            sparse_write(value, chip, h)
        return combine(inst, sparse_dot(h), zeros8)[0]

    zeros8 = jnp.zeros((8, LANES), f32)

    def inner_rows(residual, image):
        gamma = jnp.sum(own[...] * residual * residual, axis=0, keepdims=True)
        delta = jnp.sum(residual * image, axis=0, keepdims=True)
        return jnp.concatenate([gamma, delta, jnp.zeros((6, LANES), f32)], axis=0)

    def chain(h):
        gather_wait(cg.at[h], h, dense_block(cg.at[h], h))
        yield
        total, _ = combine(h, dense_dot(kh, kl, h), zeros8)
        sg[h, q] = jnp.where(left, total[:LANES], total[LANES:])
        gather_start(sg.at[h], 2 + h)
        yield
        gather_wait(sg.at[h], 2 + h, dense_block(sg.at[h], h))
        yield
        total, _ = combine(2 + h, dense_dot(fhi, flo, h), zeros8)
        base[h] = total
        mine = pick_rows(total)
        scalars = zeros8
        gamma_was = alpha_was = None
        for g in range(ITERS + 1):
            e = g * 2 + h
            if g == ITERS:
                fw[h, len(COLUMN)] = scalars
                for k, (dz, fy) in enumerate(COLUMN):
                    copy = remote(fw.at[h, len(COLUMN)], fw.at[h, k], asend.at[h, k], arecv.at[h, k], column_dev(dz, fy))
                    copy.start()
                    pending.append(copy)
                yield
                tx[h] = full_rows(12 + 3 * h, h, wx)
                tr[h] = full_rows(13 + 3 * h, h, wr)
                tp[h] = full_rows(14 + 3 * h, h, wp)
                yield
                sums = scalars
                for k, (dz, fy) in enumerate(COLUMN):
                    here = fw.at[h, k]
                    remote(here, here, asend.at[h, k], arecv.at[h, k], column_dev(dz, fy)).wait_recv()
                    sums = sums + fw[h, k]
                fg[h, q] = sums
                gather_start(fg.at[h], 12 + h)
                yield
                gather_wait(fg.at[h], 12 + h, lambda chip: None)
                sums = zeros8
                for chip in range(CHIPS):
                    sums = sums + fg[h, chip]
                fps[h] = sums
                copy = remote(fps.at[h], fpr.at[h], psend.at[18 + h], precv.at[18 + h], sibling)
                copy.start()
                pending.append(copy)
                yield
                copy.wait_recv()
                sums = sums + fpr[h]
            else:
                buf = windows[h][g]
                buf[near_slot(0, 0), 0:BAND, :] = mine
                buf[near_slot(0, 0), BAND:MSG, :] = scalars
                near_start(buf, e)
                yield
                near_wait(buf, e)
                for t in range(2):
                    for b in range(3):
                        band = slice(b * SHARE, (b + 1) * SHARE)
                        far_s[e, t, band, :] = jnp.where(
                            left_band, buf[far_places[t][b], band, :], buf[far_places[t][b + 3], band, :])
                whole = sums_far(buf, far_s.at[e], BAND)
                far_start(far_s.at[e], far_r.at[e], e)
                yield
                far_wait(far_r.at[e], e)
                pieces = []
                for b in range(3):
                    band = slice(b * SHARE, (b + 1) * SHARE)
                    sides = []
                    for r in (b, b + 3):
                        rel, inside, slot = my_places[r]
                        away = jnp.where(rel < 5, far_r[e, 1, band, :], far_r[e, 0, band, :])
                        sides.append(jnp.where(inside, buf[slot, band, :], away))
                    pieces.append(mine[band, :] - jnp.where(left_band, sides[0], sides[1]))
                vector = jnp.concatenate(pieces, axis=0)
                xg[e, q, 0:BAND, :] = vector
                xg[e, q, BAND:MSG, :] = whole + far_r[e, 0, BAND:MSG, :] + far_r[e, 1, BAND:MSG, :]
                gather_start(xg.at[e], 4 + e)
                yield
                gather_wait(xg.at[e], 4 + e, sparse_block(xg.at[e], h))
                yield
                sums = zeros8
                for chip in range(CHIPS):
                    sums = sums + xg[e, chip, BAND:MSG, :]
                applied, sums = combine_picks(4 + e, h, sums)
            if g == 0:
                vr[h] = vector
                trp[h] = applied
                mine = applied
                scalars = inner_rows(vector, mine)
                wr = {0: jnp.ones((1, LANES), f32)}
                continue
            sums = sums + swap(sums)
            gamma, delta = sums[0:1], sums[1:2]
            residual = vr[h]
            if g == 1:
                alpha = gamma / delta
                step, direction, step_image = vector, residual, applied
                wp, ws = wr, {}
            else:
                beta = gamma / gamma_was
                alpha = gamma / (delta - beta * gamma / alpha_was)
                direction = residual + beta * vp[h]
                if g < ITERS:
                    step = vector + beta * vs[h]
                    step_image = applied + beta * tsp[h]
                    wp = add(wr, wp, beta)
                    ws = add({}, ws, beta)
            if g < ITERS:
                mine = trp[h] - alpha * step_image
                residual = residual - alpha * step
                scalars = inner_rows(residual, mine)
                ws[g] = jnp.ones((1, LANES), f32)
                wx = add(wx if g > 1 else {}, wp, alpha)
                wr = add(wr, ws, -alpha)
                vr[h] = residual
                vs[h] = step
                vp[h] = direction
                trp[h] = mine
                tsp[h] = step_image
                vx[h] = alpha * direction if g == 1 else vx[h] + alpha * direction
            else:
                vx[h] += alpha * direction
                base[h] = base[h] - (tx[h] + alpha * (tr[h] + beta * tp[h]))
            gamma_was, alpha_was = gamma, alpha

    chains = (chain(0), chain(1))

    def go(which):
        next(chains[which], None)

    for copy in flex_copies:
        copy.wait()
    for copy in shared_copies:
        copy.wait_recv()
    lax.fori_loop(0, 2 * CHIPS, split_flex, 0)
    go(0)
    go(0)
    pick_columns(0)
    go(1)
    go(1)
    pick_columns(1)
    for which in (0, 0, 1, 1, 0, 1, 0, 1, 0, 0, 1, 1):
        go(which)
    for _ in range(ITERS - 2):
        for which in (0, 1, 0, 1, 0, 0, 1, 1):
            go(which)
    for which in (0, 1, 0, 1, 0, 0, 0, 1, 1, 0, 1, 1, 0, 0, 1, 1):
        go(which)

    side = low_lanes(ROWS)
    trace_out[0] = jnp.where(side, base[0], base[1])
    for b in range(3):
        band = slice(b * SHARE, (b + 1) * SHARE)
        lower, upper = vx[0, band, :], vx[1, band, :]
        sign = sgn[band, :]
        lower, upper = sign * lower, sign * upper
        mult_out[0, b] = jnp.where(left_band, lower, swap(upper))
        mult_out[0, b + 3] = jnp.where(left_band, swap(lower), upper)

    for copy in pending:
        copy.wait_send()


def settle(mult, trace, mult_out, trace_out):
    mult_out[...] = mult[...]
    trace_out[...] = trace[...]


def body(edge_mid, edge_dir, seg_mid, seg_vec, currents, flexibility, partner, edge_block):
    vmem = pl.BlockSpec(memory_space=pltpu.VMEM)
    smem = pl.BlockSpec(memory_space=pltpu.SMEM)
    dma = pltpu.SemaphoreType.DMA
    half = CHIPS * ROWS

    def room(*shape):
        return pltpu.VMEM(shape, f32)

    def short(*shape):
        return pltpu.VMEM(shape, bf16)
    both = 2 * ITERS
    scratch = [
        room(CHIPS, 8, ROWS), room(2, 8, ROWS),
        room(2, CHIPS, LANES, LANES),
        room(2, CHIPS, LANES, LANES),
        room(both, CHIPS, MSG, LANES),
        room(2, CHIPS, 8, LANES),
        room(18, LANES + 8, LANES), room(18, LANES + 8, LANES),
        room(12, MSG, LANES), room(12, MSG, LANES), room(2, 8, LANES), room(2, 8, LANES),
    ]
    scratch += [room(6, MSG, LANES)] * both
    scratch += [room(2, 16, 8, LANES), room(both, 2, MSG, LANES), room(both, 2, MSG, LANES)]
    scratch += [
        room(2, ROWS, half), short(2, ROWS, half), short(2, ROWS, half),
        short(2, ROWS, DEPTH), short(2, ROWS, DEPTH),
        short(2, PICKS, DEPTH), short(2, PICKS, DEPTH), room(2, ROWS, LANES),
        short(2, ROWS, half), short(2, ROWS, half),
        short(2, half, LANES), short(2, DEPTH, LANES),
        room(ROWS, ROWS), room(ROWS, ROWS), short(PICKS, ROWS), room(ROWS, ROWS),
        room(LANES, ROWS), room(2, 6, ROWS, LANES),
        room(BAND, LANES), room(BAND, LANES),
    ]
    scratch += [room(2, ROWS, LANES)] * 4
    scratch += [room(2, BAND, LANES)] * 6
    scratch += [
        dma((8,)), dma((8,)), dma((8,)), dma, dma, dma((7,)), dma((7,)),
        dma((14, 7)), dma((14, 7)), dma((20,)), dma((20,)),
        dma((8, 5)), dma((8, 5)), dma((8, 2)), dma((8, 2)), dma((2, 15)), dma((2, 15)),
    ]
    outs = (
        jax.ShapeDtypeStruct((1, ROUNDS, SHARE, LANES), f32),
        jax.ShapeDtypeStruct((1, ROWS, LANES), f32),
    )
    solved = pl.pallas_call(
        kernel,
        out_shape=outs,
        in_specs=[vmem] * 5 + [smem] * 2 + [pl.BlockSpec(memory_space=pl.ANY)],
        out_specs=(vmem, vmem),
        scratch_shapes=scratch,
        compiler_params=pltpu.CompilerParams(
            collective_id=0, has_side_effects=True, vmem_limit_bytes=56 * 1024 * 1024),
        name="interface_cg",
    )(jnp.transpose(edge_mid, (1, 0, 2)), jnp.transpose(edge_dir, (1, 0, 2)),
      seg_mid, seg_vec, currents, partner, edge_block, flexibility)
    return pl.pallas_call(
        settle,
        out_shape=outs,
        in_specs=[vmem] * 2,
        out_specs=(vmem, vmem),
        name="settle",
    )(*solved)


def solution(mesh):
    in_specs = (
        P("sub", None, "seg"),
        P("sub", None, "seg"),
        P(None, "seg"),
        P(None, "seg"),
        P(None, "seg"),
        P("sub", "seg", None),
        P(),
        P(None, "sub", None),
    )
    out_specs = (P("sub", None, "seg", None), P("sub", "seg", None))
    return jax.shard_map(body, mesh=mesh, in_specs=in_specs, out_specs=out_specs, check_vma=False)
```

```python
import jax
import jax.numpy as jnp
from jax import lax
from jax.experimental import pallas as pl
from jax.experimental.pallas import tpu as pltpu
from jax.sharding import PartitionSpec as P

ITERS = 4
ROUNDS = 6
SHARE = 24
PICKS = ROUNDS * SHARE
BAND = PICKS // 2
MSG = BAND + 8
ROWS = 256
LANES = 128
HALF = LANES // 2
CHIPS = 8
MAIN = CHIPS * LANES
DEPTH = CHIPS * PICKS
CORE2 = 0.05 * 0.05
f32 = jnp.float32
bf16 = jnp.bfloat16
MESH = pl.DeviceIdType.MESH

PLANE = ((2, 1), (1, 1), (-1, 1), (2, 0), (1, 0), (-1, 0), (0, 1))
NEAR = ((1, 1), (-1, 1), (0, 1), (1, 0), (-1, 0))
FAR = (3, -3)
COLUMN = tuple((dz, fy) for dz in (4, -3, 3, -2, 2, -1, 1, 0) for fy in (1, 0) if dz or fy)


def split2(value):
    high = value.astype(bf16)
    return high, (value - high.astype(f32)).astype(bf16)


def dot(a, b):
    return jnp.dot(a, b, preferred_element_type=f32)


def kernel(em, ed, sm, sv, cur, part, eb, flex,
           mult_out, trace_out,
           geo, ge, cg, sg, xg, fg, ps, pr, pps, ppr, fps, fpr,
           wa0, wa1, wa2, wa3, wb0, wb1, wb2, wb3, fw, far_s, far_r,
           fv, fhi, flo, fsh, fsl, fssh, fssl, rem, kh, kl, cb, xb, pt, pk, ptb, pb, est, ebc,
           sgn, own, base, tx, tr, tp, trp, tsp, vr, vs, vp, vx,
           fsem, fsend, frecv, esend, erecv, gsend, grecv, dsend, drecv, psend, precv,
           nsend, nrecv, zsend, zrecv, asend, arecv):
    seg = lax.axis_index("seg")
    sub = lax.axis_index("sub")
    x, ylo, c = seg // 4, (seg // 2) % 2, seg % 2
    z, yh = sub // 2, sub % 2
    q = seg // 2
    windows = ((wa0, wa1, wa2, wa3), (wb0, wb1, wb2, wb3))

    def plane_dev(dx, fy, fc):
        yy = 1 - ylo if fy else ylo
        cc = 1 - c if fc else c
        return (((x + dx + 4) % 4) * 4 + yy * 2 + cc, sub)

    def column_dev(dz, fy):
        yy = 1 - yh if fy else yh
        return (seg, ((z + dz + 8) % 8) * 2 + yy)

    def chip_from(dx, fy):
        yy = 1 - ylo if fy else ylo
        return ((x - dx + 4) % 4) * 2 + yy

    def remote(src, dst, ss, rs, dev):
        return pltpu.make_async_remote_copy(
            src_ref=src, dst_ref=dst, send_sem=ss, recv_sem=rs, device_id=dev, device_id_type=MESH)

    pending = []
    sibling = plane_dev(0, 0, 1)

    def low_lanes(rows):
        return lax.broadcasted_iota(jnp.int32, (rows, LANES), 1) < HALF

    def swap(value):
        return pltpu.roll(value, HALF, 1)

    flex_copies = []
    for chip in range(CHIPS):
        src = flex.at[0, :, pl.ds(pl.multiple_of((chip * 2 + c) * ROWS, ROWS), ROWS)]
        copy = pltpu.make_async_copy(src, fv.at[c, :, chip * ROWS:(chip + 1) * ROWS], fsem.at[chip])
        copy.start()
        flex_copies.append(copy)
    barrier = pltpu.get_barrier_semaphore()
    peers = [plane_dev(dx, fy, 0) for dx, fy in PLANE] + [sibling]
    peers += [column_dev(dz, fy) for dz, fy in COLUMN]
    for peer in peers:
        pl.semaphore_signal(barrier, inc=1, device_id=peer, device_id_type=MESH)
    geo[q, 0:3, :] = sm[...]
    geo[q, 3:6, :] = sv[...]
    geo[q, 6:8, :] = jnp.zeros((2, ROWS), f32)
    for comp in range(3):
        ge[c, comp:comp + 1, :] = em[comp]
        ge[c, 3 + comp:4 + comp, :] = ed[comp]
    ge[c, 6:8, :] = jnp.zeros((2, ROWS), f32)
    turned = cur[...].T
    left = low_lanes(LANES)
    cg[0, q] = jnp.where(left, turned[:LANES], swap(turned[LANES:]))
    cg[1, q] = jnp.where(left, swap(turned[:LANES]), turned[LANES:])
    pl.semaphore_wait(barrier, len(peers))

    edge_copy = remote(ge.at[c], ge.at[c], esend, erecv, sibling)
    edge_copy.start()
    pending.append(edge_copy)
    geo_copies = []
    for k, (dx, fy) in enumerate(PLANE):
        copy = remote(geo.at[q], geo.at[q], gsend.at[k], grecv.at[k], plane_dev(dx, fy, 0))
        copy.start()
        geo_copies.append(copy)
    pending.extend(geo_copies)

    def gather_start(buf, g):
        mine = buf.at[q]
        for k, (dx, fy) in enumerate(PLANE):
            copy = remote(mine, mine, dsend.at[g, k], drecv.at[g, k], plane_dev(dx, fy, 0))
            copy.start()
            pending.append(copy)

    def gather_wait(buf, g, each):
        each(q)
        for k, (dx, fy) in enumerate(PLANE):
            origin = chip_from(dx, fy)
            here = buf.at[origin]
            remote(here, here, dsend.at[g, k], drecv.at[g, k], sibling).wait_recv()
            each(origin)

    gather_start(cg.at[0], 0)
    gather_start(cg.at[1], 1)
    shared_copies = []
    for chip in range(CHIPS):
        src = flex.at[0, :, pl.ds(pl.multiple_of((chip * 2 + 1 - c) * ROWS, ROWS), ROWS)]
        dst = fv.at[c, :, chip * ROWS:(chip + 1) * ROWS]
        copy = remote(src, dst, fsend.at[chip], frecv.at[chip], sibling)
        copy.start()
        shared_copies.append(copy)
    pending.extend(shared_copies)

    lane_at = lax.broadcasted_iota(jnp.int32, (1, ROWS), 1)
    pt[...] = jnp.zeros((ROWS, ROWS), f32)
    pk[...] = jnp.zeros((ROWS, ROWS), f32)

    def hot_row(k, carry):
        row = jnp.where(lane_at == eb[k // SHARE, 0, k % SHARE], 1.0, 0.0).astype(f32)
        upper = k // BAND
        at = k - upper * BAND
        place = jnp.where(at < HALF, upper * HALF + at, LANES + upper * 8 + at - HALF)
        pt[pl.ds(k, 1), :] = row
        pk[pl.ds(place, 1), :] = row
        return carry
    lax.fori_loop(0, PICKS, hot_row, 0)
    ptb[...] = pt[0:PICKS, :].astype(bf16)
    pb[...] = pk[...].T

    edge_copy.wait_recv()
    for side in range(2):
        est[...] = jnp.zeros((LANES, ROWS), f32)
        est[0:8, :] = ge[side]
        columns = est[...].T
        for comp in range(6):
            ebc[side, comp] = jnp.broadcast_to(columns[:, comp:comp + 1], (ROWS, LANES))

    left_band = low_lanes(SHARE)
    for b in range(3):
        band = slice(b * SHARE, (b + 1) * SHARE)
        first = jnp.where(part[b, sub] > sub, 1.0, 0.0).astype(f32)
        second = jnp.where(part[b + 3, sub] > sub, 1.0, 0.0).astype(f32)
        mark = jnp.where(left_band, first, second)
        own[band, :] = mark
        sgn[band, :] = mark * 2.0 - 1.0

    for copy in geo_copies:
        copy.wait_recv()

    def tile(step, carry):
        side, chip = step // CHIPS, step % CHIPS
        for h in range(2):
            row = [geo[chip, pl.ds(comp, 1), h * LANES:(h + 1) * LANES] for comp in range(6)]
            lanes = pl.ds(pl.multiple_of(chip * ROWS + h * LANES, LANES), LANES)
            for part_at in range(4):
                rows = slice(part_at * 64, part_at * 64 + 64)
                dist = jnp.full((64, LANES), CORE2, f32)
                along = jnp.zeros((64, LANES), f32)
                for comp in range(3):
                    gap = ebc[side, comp, rows, :] - row[comp]
                    dist = dist + gap * gap
                    along = along + ebc[side, 3 + comp, rows, :] * row[3 + comp]
                high, low = split2(along * lax.rsqrt(dist))
                kh[side, rows, lanes] = high
                kl[side, rows, lanes] = low
        return carry
    lax.fori_loop(0, 2 * CHIPS, tile, 0)

    def unpack(value):
        high = value.astype(bf16).astype(f32)
        low = value - high
        side = low_lanes(value.shape[0])
        return jnp.where(side, high, swap(low)), jnp.where(side, swap(high), low)

    def dense_block(buf, h):
        def each(chip):
            one, two = unpack(buf[chip])
            cb[h, pl.ds(pl.multiple_of(chip * ROWS, LANES), LANES), :] = one.astype(bf16)
            cb[h, pl.ds(pl.multiple_of(chip * ROWS + LANES, LANES), LANES), :] = two.astype(bf16)
        return each

    def dense_dot(high, low, h):
        def rows_of(side):
            return dot(high[side], cb[h]) + dot(low[side], cb[h])
        return rows_of

    def combine(inst, rows_of, scalars):
        other = rows_of(1 - c)
        other = other + swap(other)
        ps[inst, 0:LANES, :] = jnp.where(left, other[:LANES], other[LANES:])
        ps[inst, LANES:LANES + 8, :] = scalars
        copy = remote(ps.at[inst], pr.at[inst], psend.at[inst], precv.at[inst], sibling)
        copy.start()
        pending.append(copy)
        mine = rows_of(c)
        mine = mine + swap(mine)
        copy.wait_recv()
        got = pr[inst, 0:LANES, :]
        back = swap(got)
        top = mine[:LANES] + jnp.where(left, got, back)
        bottom = mine[LANES:] + jnp.where(left, back, got)
        return jnp.concatenate([top, bottom], axis=0), scalars + pr[inst, LANES:LANES + 8, :]

    def split_flex(step, carry):
        side, chip = step // CHIPS, step % CHIPS
        for h in range(2):
            lanes = pl.ds(pl.multiple_of(chip * ROWS + h * LANES, LANES), LANES)
            high, low = split2(fv[side, :, lanes])
            fhi[side, :, lanes] = high
            flo[side, :, lanes] = low
        return carry

    def pick_columns(half):
        rem[...] = jnp.zeros((2, ROWS, LANES), f32)

        def one(chip, carry):
            tail = pltpu.roll(pb[:, LANES:], chip * (PICKS - LANES), 1)
            choose = jnp.concatenate([pb[:, :LANES], tail], axis=1).astype(bf16)
            src = pl.ds(pl.multiple_of(chip * ROWS, ROWS), ROWS)
            dst = pl.ds(pl.multiple_of(chip * LANES, LANES), LANES)
            for at, (whole, out) in enumerate(((fhi, fsh), (flo, fsl))):
                got = dot(whole[half, :, src], choose)
                out[half, :, dst] = got[:, :LANES].astype(bf16)
                rem[at] += got[:, LANES:]
            return carry
        lax.fori_loop(0, CHIPS, one, 0)
        fsh[half, :, MAIN:] = rem[0].astype(bf16)
        fsl[half, :, MAIN:] = rem[1].astype(bf16)
        fssh[half] = dot(ptb[...], fsh[half]).astype(bf16)
        fssl[half] = dot(ptb[...], fsl[half]).astype(bf16)

    def pick_rows(full):
        high = full.astype(bf16)
        rest = full - high.astype(f32)
        mid = rest.astype(bf16)
        low = (rest - mid.astype(f32)).astype(bf16)
        both = dot(ptb[...], jnp.where(low_lanes(ROWS), high.astype(f32), mid.astype(f32)).astype(bf16))
        picked = (both + swap(both)) + dot(ptb[...], low)
        return jnp.where(low_lanes(BAND), picked[:BAND], picked[BAND:])

    def near_slot(dz, fy):
        return (dz + 1) * 2 + fy

    def near_start(buf, e):
        mine = buf.at[near_slot(0, 0)]
        for k, (dz, fy) in enumerate(NEAR):
            copy = remote(mine, buf.at[near_slot(-dz, fy)], nsend.at[e, k], nrecv.at[e, k], column_dev(dz, fy))
            copy.start()
            pending.append(copy)

    def near_wait(buf, e):
        for k, (dz, fy) in enumerate(NEAR):
            here = buf.at[near_slot(-dz, fy)]
            remote(here, here, nsend.at[e, k], nrecv.at[e, k], column_dev(dz, fy)).wait_recv()

    def far_start(src, dst, e):
        for t, dz in enumerate(FAR):
            copy = remote(src.at[t], dst.at[t], zsend.at[e, t], zrecv.at[e, t], column_dev(dz, 0))
            copy.start()
            pending.append(copy)

    def far_wait(dst, e):
        for t, dz in enumerate(FAR):
            here = dst.at[t]
            remote(here, here, zsend.at[e, t], zrecv.at[e, t], column_dev(dz, 0)).wait_recv()

    def place_of(r, at):
        p = part[r, at]
        rel = (p // 2 - z + 8) % 8
        shifted = (rel + 1) % 8
        slot = shifted * 2 + jnp.where(p % 2 == yh, 0, 1)
        inside = shifted < 3
        return rel, inside, jnp.where(inside, slot, 0)

    far_places = [[place_of(r, ((z + dz + 8) % 8) * 2 + yh)[2] for r in range(ROUNDS)] for dz in FAR]
    my_places = [place_of(r, sub) for r in range(ROUNDS)]

    def sums_far(buf, dst, at):
        keep = [buf[s, at:at + 8, :] for s in range(6)]
        upper = (keep[2] + keep[3]) + (keep[4] + keep[5])
        whole = upper + (keep[0] + keep[1])
        dst[0, at:at + 8, :] = upper
        dst[1, at:at + 8, :] = whole
        return whole

    def sparse_write(packed, chip, h):
        one, two = unpack(packed)
        for at, value in ((0, one), (HALF, two)):
            rows = pl.ds(pl.multiple_of(chip * LANES + at, HALF), HALF)
            xb[h, rows, :] = value[:HALF].astype(bf16)
        tail = pl.ds(pl.multiple_of(MAIN + chip * 16, 16), 16)
        xb[h, tail, :] = jnp.concatenate([one[HALF:], two[HALF:]], axis=0).astype(bf16)

    def sparse_block(buf, h):
        def each(chip):
            sparse_write(buf[chip, 0:BAND, :], chip, h)
        return each

    def sparse_dot(h):
        def rows_of(side):
            return dot(fsh[side], xb[h]) + dot(fsl[side], xb[h])
        return rows_of

    def combine_picks(inst, h, scalars):
        left_pack = low_lanes(BAND)

        def rows_of(side):
            got = dot(fssh[side], xb[h]) + dot(fssl[side], xb[h])
            got = got + swap(got)
            return jnp.where(left_pack, got[:BAND], got[BAND:])
        pps[inst, 0:BAND, :] = rows_of(1 - c)
        pps[inst, BAND:MSG, :] = scalars
        copy = remote(pps.at[inst], ppr.at[inst], psend.at[inst], precv.at[inst], sibling)
        copy.start()
        pending.append(copy)
        mine = rows_of(c)
        copy.wait_recv()
        return mine + ppr[inst, 0:BAND, :], scalars + ppr[inst, BAND:MSG, :]

    def add(first, second, scale):
        out = dict(first)
        for key, value in second.items():
            out[key] = out[key] + scale * value if key in out else scale * value
        return out

    def full_rows(inst, h, weights):
        for chip in range(CHIPS):
            value = None
            for g, weight in weights.items():
                term = weight * xg[g * 2 + h, chip, 0:BAND, :]
                value = term if value is None else value + term
            sparse_write(value, chip, h)
        return combine(inst, sparse_dot(h), zeros8)[0]

    zeros8 = jnp.zeros((8, LANES), f32)

    def inner_rows(residual, image):
        gamma = jnp.sum(own[...] * residual * residual, axis=0, keepdims=True)
        delta = jnp.sum(residual * image, axis=0, keepdims=True)
        return jnp.concatenate([gamma, delta, jnp.zeros((6, LANES), f32)], axis=0)

    def chain(h):
        gather_wait(cg.at[h], h, dense_block(cg.at[h], h))
        yield
        total, _ = combine(h, dense_dot(kh, kl, h), zeros8)
        sg[h, q] = jnp.where(left, total[:LANES], total[LANES:])
        gather_start(sg.at[h], 2 + h)
        yield
        gather_wait(sg.at[h], 2 + h, dense_block(sg.at[h], h))
        yield
        total, _ = combine(2 + h, dense_dot(fhi, flo, h), zeros8)
        base[h] = total
        mine = pick_rows(total)
        scalars = zeros8
        gamma_was = alpha_was = None
        for g in range(ITERS + 1):
            e = g * 2 + h
            if g == ITERS:
                fw[h, len(COLUMN)] = scalars
                for k, (dz, fy) in enumerate(COLUMN):
                    copy = remote(fw.at[h, len(COLUMN)], fw.at[h, k], asend.at[h, k], arecv.at[h, k], column_dev(dz, fy))
                    copy.start()
                    pending.append(copy)
                yield
                tx[h] = full_rows(12 + 3 * h, h, wx)
                tr[h] = full_rows(13 + 3 * h, h, wr)
                tp[h] = full_rows(14 + 3 * h, h, wp)
                yield
                sums = scalars
                for k, (dz, fy) in enumerate(COLUMN):
                    here = fw.at[h, k]
                    remote(here, here, asend.at[h, k], arecv.at[h, k], column_dev(dz, fy)).wait_recv()
                    sums = sums + fw[h, k]
                fg[h, q] = sums
                gather_start(fg.at[h], 12 + h)
                yield
                gather_wait(fg.at[h], 12 + h, lambda chip: None)
                sums = zeros8
                for chip in range(CHIPS):
                    sums = sums + fg[h, chip]
                fps[h] = sums
                copy = remote(fps.at[h], fpr.at[h], psend.at[18 + h], precv.at[18 + h], sibling)
                copy.start()
                pending.append(copy)
                yield
                copy.wait_recv()
                sums = sums + fpr[h]
            else:
                buf = windows[h][g]
                buf[near_slot(0, 0), 0:BAND, :] = mine
                buf[near_slot(0, 0), BAND:MSG, :] = scalars
                near_start(buf, e)
                yield
                near_wait(buf, e)
                for t in range(2):
                    for b in range(3):
                        band = slice(b * SHARE, (b + 1) * SHARE)
                        far_s[e, t, band, :] = jnp.where(
                            left_band, buf[far_places[t][b], band, :], buf[far_places[t][b + 3], band, :])
                whole = sums_far(buf, far_s.at[e], BAND)
                far_start(far_s.at[e], far_r.at[e], e)
                yield
                far_wait(far_r.at[e], e)
                pieces = []
                for b in range(3):
                    band = slice(b * SHARE, (b + 1) * SHARE)
                    sides = []
                    for r in (b, b + 3):
                        rel, inside, slot = my_places[r]
                        away = jnp.where(rel < 5, far_r[e, 1, band, :], far_r[e, 0, band, :])
                        sides.append(jnp.where(inside, buf[slot, band, :], away))
                    pieces.append(mine[band, :] - jnp.where(left_band, sides[0], sides[1]))
                vector = jnp.concatenate(pieces, axis=0)
                xg[e, q, 0:BAND, :] = vector
                xg[e, q, BAND:MSG, :] = whole + far_r[e, 0, BAND:MSG, :] + far_r[e, 1, BAND:MSG, :]
                gather_start(xg.at[e], 4 + e)
                yield
                gather_wait(xg.at[e], 4 + e, sparse_block(xg.at[e], h))
                yield
                sums = zeros8
                for chip in range(CHIPS):
                    sums = sums + xg[e, chip, BAND:MSG, :]
                applied, sums = combine_picks(4 + e, h, sums)
            if g == 0:
                vr[h] = vector
                trp[h] = applied
                mine = applied
                scalars = inner_rows(vector, mine)
                wr = {0: jnp.ones((1, LANES), f32)}
                continue
            sums = sums + swap(sums)
            gamma, delta = sums[0:1], sums[1:2]
            residual = vr[h]
            if g == 1:
                alpha = gamma / delta
                step, direction, step_image = vector, residual, applied
                wp, ws = wr, {}
            else:
                beta = gamma / gamma_was
                alpha = gamma / (delta - beta * gamma / alpha_was)
                direction = residual + beta * vp[h]
                if g < ITERS:
                    step = vector + beta * vs[h]
                    step_image = applied + beta * tsp[h]
                    wp = add(wr, wp, beta)
                    ws = add({}, ws, beta)
            if g < ITERS:
                mine = trp[h] - alpha * step_image
                residual = residual - alpha * step
                scalars = inner_rows(residual, mine)
                ws[g] = jnp.ones((1, LANES), f32)
                wx = add(wx if g > 1 else {}, wp, alpha)
                wr = add(wr, ws, -alpha)
                vr[h] = residual
                vs[h] = step
                vp[h] = direction
                trp[h] = mine
                tsp[h] = step_image
                vx[h] = alpha * direction if g == 1 else vx[h] + alpha * direction
            else:
                vx[h] += alpha * direction
                base[h] = base[h] - (tx[h] + alpha * (tr[h] + beta * tp[h]))
            gamma_was, alpha_was = gamma, alpha

    chains = (chain(0), chain(1))

    def go(which):
        next(chains[which], None)

    for copy in flex_copies:
        copy.wait()
    for copy in shared_copies:
        copy.wait_recv()
    lax.fori_loop(0, 2 * CHIPS, split_flex, 0)
    go(0)
    go(0)
    pick_columns(0)
    go(1)
    go(1)
    pick_columns(1)
    for which in (0, 0, 1, 1, 0, 1, 0, 1, 0, 0, 1, 1):
        go(which)
    for _ in range(ITERS - 2):
        for which in (0, 1, 0, 1, 0, 0, 1, 1):
            go(which)
    for which in (0, 1, 0, 1, 0, 0, 0, 1, 1, 0, 1, 1, 0, 0, 1, 1):
        go(which)

    side = low_lanes(ROWS)
    trace_out[0] = jnp.where(side, base[0], base[1])
    for b in range(3):
        band = slice(b * SHARE, (b + 1) * SHARE)
        lower, upper = vx[0, band, :], vx[1, band, :]
        sign = sgn[band, :]
        lower, upper = sign * lower, sign * upper
        mult_out[0, b] = jnp.where(left_band, lower, swap(upper))
        mult_out[0, b + 3] = jnp.where(left_band, swap(lower), upper)

    for copy in pending:
        copy.wait_send()


def settle(mult, trace, mult_out, trace_out):
    mult_out[...] = mult[...]
    trace_out[...] = trace[...]


def body(edge_mid, edge_dir, seg_mid, seg_vec, currents, flexibility, partner, edge_block):
    vmem = pl.BlockSpec(memory_space=pltpu.VMEM)
    smem = pl.BlockSpec(memory_space=pltpu.SMEM)
    dma = pltpu.SemaphoreType.DMA
    half = CHIPS * ROWS

    def room(*shape):
        return pltpu.VMEM(shape, f32)

    def short(*shape):
        return pltpu.VMEM(shape, bf16)
    both = 2 * ITERS
    scratch = [
        room(CHIPS, 8, ROWS), room(2, 8, ROWS),
        room(2, CHIPS, LANES, LANES),
        room(2, CHIPS, LANES, LANES),
        room(both, CHIPS, MSG, LANES),
        room(2, CHIPS, 8, LANES),
        room(18, LANES + 8, LANES), room(18, LANES + 8, LANES),
        room(12, MSG, LANES), room(12, MSG, LANES), room(2, 8, LANES), room(2, 8, LANES),
    ]
    scratch += [room(6, MSG, LANES)] * both
    scratch += [room(2, 16, 8, LANES), room(both, 2, MSG, LANES), room(both, 2, MSG, LANES)]
    scratch += [
        room(2, ROWS, half), short(2, ROWS, half), short(2, ROWS, half),
        short(2, ROWS, DEPTH), short(2, ROWS, DEPTH),
        short(2, PICKS, DEPTH), short(2, PICKS, DEPTH), room(2, ROWS, LANES),
        short(2, ROWS, half), short(2, ROWS, half),
        short(2, half, LANES), short(2, DEPTH, LANES),
        room(ROWS, ROWS), room(ROWS, ROWS), short(PICKS, ROWS), room(ROWS, ROWS),
        room(LANES, ROWS), room(2, 6, ROWS, LANES),
        room(BAND, LANES), room(BAND, LANES),
    ]
    scratch += [room(2, ROWS, LANES)] * 4
    scratch += [room(2, BAND, LANES)] * 6
    scratch += [
        dma((8,)), dma((8,)), dma((8,)), dma, dma, dma((7,)), dma((7,)),
        dma((14, 7)), dma((14, 7)), dma((20,)), dma((20,)),
        dma((8, 5)), dma((8, 5)), dma((8, 2)), dma((8, 2)), dma((2, 15)), dma((2, 15)),
    ]
    outs = (
        jax.ShapeDtypeStruct((1, ROUNDS, SHARE, LANES), f32),
        jax.ShapeDtypeStruct((1, ROWS, LANES), f32),
    )
    solved = pl.pallas_call(
        kernel,
        out_shape=outs,
        in_specs=[vmem] * 5 + [smem] * 2 + [pl.BlockSpec(memory_space=pl.ANY)],
        out_specs=(vmem, vmem),
        scratch_shapes=scratch,
        compiler_params=pltpu.CompilerParams(
            collective_id=0, has_side_effects=True, vmem_limit_bytes=56 * 1024 * 1024),
        name="interface_cg",
    )(jnp.transpose(edge_mid, (1, 0, 2)), jnp.transpose(edge_dir, (1, 0, 2)),
      seg_mid, seg_vec, currents, partner, edge_block, flexibility)
    return pl.pallas_call(
        settle,
        out_shape=outs,
        in_specs=[vmem] * 2,
        out_specs=(vmem, vmem),
        name="settle",
    )(*solved)


def solution(mesh):
    in_specs = (
        P("sub", None, "seg"),
        P("sub", None, "seg"),
        P(None, "seg"),
        P(None, "seg"),
        P(None, "seg"),
        P("sub", "seg", None),
        P(),
        P(None, "sub", None),
    )
    out_specs = (P("sub", None, "seg", None), P("sub", "seg", None))
    return jax.shard_map(body, mesh=mesh, in_specs=in_specs, out_specs=out_specs, check_vma=False)
```
